512 devices in a mesh: gx: 16 (over z), gy: 32 (over x, y, core).
Axes of the slice: x: 4, y: 4, z: 16, core: 2. Of those that a mesh axis runs over, the one named last changes fastest.
Arguments:
- right_side: float32 [128, 512, 128], P('gx', 'gy'), may hold values from -8 to 8
- diagonal: float32 [128, 512, 128], P('gx', 'gy'), may hold values from 0.25 to 2
- solid_mask: int32 [128, 512, 128], P('gx', 'gy'), may hold values 0 or 1
- geneo_vectors: bfloat16 [32, 128, 512, 128], P(None, 'gx', 'gy'), may hold values from -0.046875 to 0.046875
- vector_counts: int32 [16, 32], P('gx', 'gy'), may hold values from 8 to 32, as said below
- owner_slots: int32 [512], replicated, may hold values from 0 to 511, each once
- coarse_inverse: float32 [16384, 1024], P('gy'), may hold values from -1 to 8, as said below
Outputs:
- solution: float32 [128, 512, 128], P('gx', 'gy')
- residual: float32 [128, 512, 128], P('gx', 'gy')
The draws below stay inside these ranges and needn't reach their ends.
Inputs may be any that keep to these rules, and one draw needn't show every extreme that they name: `vector_counts`: every count lies between 8 and 32; both ends occur in every draw. Subdomain s belongs to coarse block owner_slots[s] // 32. `coarse_inverse`: each block is symmetric positive definite; rows and columns beyond a subdomain's count are unused.
All inputs are finite; a program needn't handle non-finite values. No bound on the sum of `solid_mask` on one device may be relied on, other than what follows from the above.
Results may differ from the reference program's by a relative error of at most 0.0003.
Values sent between devices are 32-bit elements; how exact they have to be, the bound alone decides.
A program may use at most 64 MiB of HBM per device.

```python
import jax
import jax.numpy as jnp
from jax import lax

CX = 8
CY = 16
CZ = 128
KMAX = 32
OWNERS = 16
DEG = 3
ITERS = 2
SUBX = 16
SUBY = 32
NSUB = 512
BLK = 1024
NX = 128
NY = 512


def draw_vector_counts(key, part):
    total = SUBX * SUBY
    values = jax.random.randint(key, (total,), KMAX // 4, KMAX + 1)
    where = jax.random.randint(jax.random.fold_in(key, 1), (), 0, total)
    values = values.at[where].set(KMAX)
    values = values.at[(where + 1) % total].set(KMAX // 4)
    return values.reshape(SUBX, SUBY).astype(jnp.int32)


def draw_coarse_inverse(key, part):
    spread = jax.random.uniform(key, (OWNERS, BLK, BLK), jnp.float32, -1.0, 1.0) / jnp.sqrt(jnp.float32(BLK))
    sym = 0.5 * (spread + jnp.swapaxes(spread, 1, 2))
    diag_vals = jax.random.uniform(jax.random.fold_in(key, 2), (OWNERS, BLK), jnp.float32, 2.0, 4.0)
    index = jnp.arange(BLK)
    eye_mat = (index[:, None] == index[None, :]).astype(jnp.float32)
    whole = sym * (1.0 - eye_mat)[None] + eye_mat[None] * diag_vals[:, :, None]
    return whole.reshape(OWNERS * BLK, BLK)


def touch_ends(result, rng, low, largest):
    longest = result.shape.index(max(result.shape))
    spots = []
    for shift in (0, 1):
        where = [jax.random.randint(jax.random.fold_in(rng, axis), (), 0, length) for axis, length in enumerate(result.shape)]
        where[longest] = (where[longest] + shift) % result.shape[longest]
        spots.append(tuple(where))
    return result.at[spots[0]].set(low).at[spots[1]].set(largest)


def levels(rng, dims, pieces, least, largest):
    def one(dim, parts):
        steps = jax.random.uniform(jax.random.fold_in(jax.random.fold_in(rng, 6), dim), (parts,), jnp.float32, least / len(pieces), largest / len(pieces))
        return jnp.repeat(jnp.exp(steps), dims[dim] // parts).reshape((-1,) + (1,) * (len(dims) - dim - 1))

    loudness = one(*pieces[0])
    for cut in pieces[1:]:
        loudness = loudness * one(*cut)
    return loudness


def centred(key, dims, scale, bound, split=(), held_as=jnp.bfloat16):
    result = jax.random.normal(key, dims, jnp.float32) * scale
    if len(split) > 0:
        result = levels(key, dims, split, -0.22, 0.18) * result
    return jnp.clip(result, min=-bound, max=bound).astype(held_as)


def setup_inputs(seed: int = 0) -> dict:
    keys = jax.random.split(jax.random.key(seed), 8)
    right_side = centred(keys[0], (NX, NY, CZ), 1.0, 8.0, ((0, 16), (1, 32)), jnp.float32)
    diagonal = jnp.clip(0.25 + 1.75 * jax.random.uniform(keys[1], (NX, NY, CZ), jnp.float32) ** levels(keys[1], (NX, NY, CZ), ((0, 16), (1, 32)), -0.2, 0.2), 0.25, 2.0)
    solid_mask = touch_ends((jax.random.randint(keys[2], (NX, NY, CZ), 0, 8) < 1).astype(jnp.int32), jax.random.fold_in(keys[2], 1), 0, 1)
    geneo_vectors = centred(keys[3], (KMAX, NX, NY, CZ), (CX * CY * CZ) ** -0.5, 0.046875, ((1, 16), (2, 32)))
    vector_counts = draw_vector_counts(jax.random.fold_in(keys[7], 71), 0)
    owner_slots = jax.random.permutation(keys[5], NSUB).astype(jnp.int32)
    coarse_inverse = draw_coarse_inverse(jax.random.fold_in(keys[7], 71), 0)
    return {"right_side": right_side, "diagonal": diagonal, "solid_mask": solid_mask, "geneo_vectors": geneo_vectors, "vector_counts": vector_counts, "owner_slots": owner_slots, "coarse_inverse": coarse_inverse}


CHEB_LO = 0.3
CHEB_HI = 2.0
HIGH = lax.Precision.HIGHEST


def operate(field, diagonal, fluid):
    masked = fluid * field
    padded = jnp.pad(masked, 1)
    beside = padded[2:, 1:-1, 1:-1] + padded[:-2, 1:-1, 1:-1]
    beside = beside + padded[1:-1, 2:, 1:-1] + padded[1:-1, :-2, 1:-1]
    beside = beside + padded[1:-1, 1:-1, 2:] + padded[1:-1, 1:-1, :-2]
    return fluid * ((6.0 + diagonal) * field - beside) + (1.0 - fluid) * field


def smoother(res, diagonal, fluid, jacobi):
    centre = (CHEB_HI + CHEB_LO) / 2.0
    half_width = (CHEB_HI - CHEB_LO) / 2.0
    sigma_val = centre / half_width
    rho_old = 1.0 / sigma_val
    update = jacobi * res / centre
    smooth = update
    remainder = res
    for repeat in range(DEG - 1):
        remainder = remainder - operate(update, diagonal, fluid)
        rho_new = 1.0 / (2.0 * sigma_val - rho_old)
        update = rho_new * rho_old * update + (2.0 * rho_new / half_width) * jacobi * remainder
        smooth = smooth + update
        rho_old = rho_new
    return smooth


def reference(right_side, diagonal, solid_mask, geneo_vectors, vector_counts, owner_slots, coarse_inverse):
    fluid = 1.0 - solid_mask.astype(jnp.float32)
    jacobi = 1.0 / (fluid * (6.0 + diagonal) + 1.0 - fluid)
    live = (jnp.arange(KMAX, dtype=jnp.int32)[None, None, :] < vector_counts[:, :, None]).astype(jnp.float32)
    vectors = jnp.moveaxis(geneo_vectors.reshape(KMAX, SUBX, CX, SUBY, CY, CZ), 1, 0)
    inverse = coarse_inverse.reshape(OWNERS, BLK, BLK)

    def project_row(items):
        zrow, rrow = items
        return jnp.einsum("kaybz,aybz->yk", zrow.astype(jnp.float32), rrow, precision=HIGH)

    def prolong_row(items):
        zrow, crow = items
        return jnp.einsum("kaybz,yk->aybz", zrow.astype(jnp.float32), crow, precision=HIGH)

    def precondition(res):
        smooth = smoother(res, diagonal, fluid, jacobi)
        rows = res.reshape(SUBX, CX, SUBY, CY, CZ)
        projected = lax.map(project_row, (vectors, rows)) * live
        ordered = jnp.zeros((NSUB, KMAX), jnp.float32).at[owner_slots].set(projected.reshape(NSUB, KMAX))
        coarse = jnp.einsum("obc,oc->ob", inverse, ordered.reshape(OWNERS, BLK), precision=HIGH)
        coeffs = coarse.reshape(NSUB, KMAX)[owner_slots].reshape(SUBX, SUBY, KMAX) * live
        fine = lax.map(prolong_row, (vectors, coeffs))
        return smooth + fine.reshape(NX, NY, CZ)

    solution = jnp.zeros_like(right_side)
    residual = right_side
    precond = precondition(residual)
    direction = precond
    norm_now = jnp.sum(residual * precond)
    for repeat in range(ITERS):
        image = operate(direction, diagonal, fluid)
        step_len = norm_now / jnp.sum(direction * image)
        solution = solution + step_len * direction
        residual = residual - step_len * image
        if repeat + 1 < ITERS:
            precond = precondition(residual)
            norm_next = jnp.sum(residual * precond)
            direction = precond + (norm_next / norm_now) * direction
            norm_now = norm_next
    return solution, residual
```

```python
import functools

import jax
import jax.numpy as jnp
from jax import lax
from jax.experimental import pallas as pl
from jax.experimental.pallas import tpu as pltpu
from jax.sharding import PartitionSpec as P

CHEB_LO = 0.3
CHEB_HI = 2.0
THETA = (CHEB_HI + CHEB_LO) / 2.0
DELTA = (CHEB_HI - CHEB_LO) / 2.0
SIGMA = THETA / DELTA
HIGH = lax.Precision.HIGHEST
MESH = pl.DeviceIdType.MESH
F32 = jnp.float32


def lane_ids(shape):
    return lax.broadcasted_iota(jnp.int32, shape, len(shape) - 1)


def row_sums(rows):
    return lax.dot_general(
        jnp.ones((8, 128), F32), rows, (((1,), (1,)), ((), ())),
        precision=HIGH, preferred_element_type=F32,
    )


def kernel(
    nx, ny, kmax,
    right_hbm, diag_hbm, mask_hbm, vec_hbm, count_ref, slot_ref, slots_ref, inv_hbm,
    sol_ref, res_ref,
    right, diag, solid, vec, inv, fluid, jac, pad,
    parts, stack, onehot,
    zsend, zbuf, psend, pbuf, csend, cbuf,
    xsend, xbuf, ysend, ybuf,
    fsend, fzbuf, fpsend, fpbuf,
    load_sem, z_send_sem, z_recv_sem, p_send_sem, p_recv_sem, c_send_sem, c_recv_sem,
    h_send_sem, h_recv_sem, f_send_sem, f_recv_sem,
):
    gx, gy = lax.axis_index("gx"), lax.axis_index("gy")

    def along_x(step):
        return {"gx": lax.rem(gx + step, nx)}

    def along_y(step):
        return {"gy": lax.rem(gy + step, ny)}

    barrier = pltpu.get_barrier_semaphore()
    for step in range(1, nx):
        pl.semaphore_signal(barrier, inc=1, device_id=along_x(step), device_id_type=MESH)
    for step in range(1, ny):
        pl.semaphore_signal(barrier, inc=1, device_id=along_y(step), device_id_type=MESH)

    loads = [
        pltpu.make_async_copy(src, dst, load_sem.at[i])
        for i, (src, dst) in enumerate(
            [(right_hbm, right), (vec_hbm, vec), (mask_hbm, solid), (diag_hbm, diag), (inv_hbm, inv)]
        )
    ]
    for load in loads:
        load.start()

    count = count_ref[0, 0]
    lane = lane_ids((1, 128))
    live = ((lane < count) | (lane >= kmax)).astype(F32)

    def remote(src, dst, send_sem, recv_sem, device):
        return pltpu.make_async_remote_copy(
            src_ref=src, dst_ref=dst, send_sem=send_sem, recv_sem=recv_sem,
            device_id=device, device_id_type=MESH,
        )

    def wait_bytes(ref, sem):
        pltpu.make_async_copy(ref, ref, sem).wait()

    def fold(cells):
        total = jnp.sum(cells, axis=0)
        return total[0:8] + total[8:16]

    def z_start(n):
        for step in range(1, nx):
            remote(zsend.at[n], zbuf.at[n, gx], z_send_sem.at[n], z_recv_sem.at[n], along_x(step)).start()
        pltpu.make_async_copy(zsend.at[n], zbuf.at[n, gx], z_recv_sem.at[n]).start()

    def p_start(n):
        for step in range(1, ny):
            remote(psend.at[n], pbuf.at[n, :, pl.ds(gy, 1)], p_send_sem.at[n], p_recv_sem.at[n], along_y(step)).start()
        pltpu.make_async_copy(psend.at[n], pbuf.at[n, :, pl.ds(gy, 1)], p_recv_sem.at[n]).start()

    def c_start(n):
        for step in range(1, ny):
            remote(csend.at[n], cbuf.at[n, gy], c_send_sem.at[n], c_recv_sem.at[n], along_y(step)).start()
        pltpu.make_async_copy(csend.at[n], cbuf.at[n, gy], c_recv_sem.at[n]).start()

    def halo_copies(n):
        return [
            remote(xsend.at[n, 0], xbuf.at[n, 1], h_send_sem.at[n, 0], h_recv_sem.at[n, 0], along_x(nx - 1)),
            remote(xsend.at[n, 1], xbuf.at[n, 0], h_send_sem.at[n, 1], h_recv_sem.at[n, 1], along_x(1)),
            remote(ysend.at[n, 0], ybuf.at[n, 1], h_send_sem.at[n, 2], h_recv_sem.at[n, 2], along_y(ny - 1)),
            remote(ysend.at[n, 1], ybuf.at[n, 0], h_send_sem.at[n, 3], h_recv_sem.at[n, 3], along_y(1)),
        ]

    def halo_start(n, field):
        masked = fluid[...] * field
        pad[1:9, 8:24, :] = masked
        xsend[n, 0] = masked[0]
        xsend[n, 1] = masked[7]
        ysend[n, 0] = masked[:, 0, :]
        ysend[n, 1] = masked[:, 15, :]
        for copy in halo_copies(n):
            copy.start()

    def halo_finish(n, field):
        for copy in halo_copies(n):
            copy.wait_recv()
        zero = jnp.float32(0.0)
        keep = [gx > 0, gx < nx - 1, gy > 0, gy < ny - 1]
        scale = [jnp.where(k, jnp.float32(1.0), zero) for k in keep]
        pad[0, 8:24, :] = xbuf[n, 0] * scale[0]
        pad[9, 8:24, :] = xbuf[n, 1] * scale[1]
        pad[1:9, 7:8, :] = (ybuf[n, 0] * scale[2]).reshape(8, 1, 128)
        pad[1:9, 24:25, :] = (ybuf[n, 1] * scale[3]).reshape(8, 1, 128)
        masked = pad[1:9, 8:24, :]
        beside = pad[2:10, 8:24, :] + pad[0:8, 8:24, :]
        beside = beside + pad[1:9, 9:25, :] + pad[1:9, 7:23, :]
        lanes = lane_ids((8, 16, 128))
        beside = beside + jnp.where(lanes == 127, zero, pltpu.roll(masked, 127, 2))
        beside = beside + jnp.where(lanes == 0, zero, pltpu.roll(masked, 1, 2))
        fl = fluid[...]
        return fl * ((6.0 + diag[...]) * field - beside) + (1.0 - fl) * field

    def project(n, cells_ref, extras):
        def group(g, carry):
            cells = cells_ref[...]
            for j in range(4):
                k = g * 4 + j
                parts[k] = fold(vec[k].astype(F32) * cells)
            return carry

        lax.fori_loop(0, kmax // 4, group, 0)
        for i in range(8):
            parts[kmax + i] = extras[i] if i < len(extras) else jnp.zeros((8, 128), F32)
        stack[0:kmax + 8, :] = jnp.sum(parts[...], axis=1)
        zsend[n] = row_sums(stack[...])[0:1] * live

    def compact(n):
        rows = zbuf[n].reshape(nx, 128)
        low = jnp.where(lane_ids((nx, 128)) < kmax, rows, 0.0)
        packed = low[0:4]
        for a in range(1, 4):
            packed = packed + pltpu.roll(low[4 * a:4 * a + 4], 32 * a, 1)
        psend[n, 0:4] = packed.reshape(4, 1, 128)
        psend[n, 4] = jnp.sum(rows, axis=0, keepdims=True)

    def coarse(n):
        gathered = pbuf[n, 0:4].reshape(4 * ny, 128)
        picked = jnp.dot(onehot[...], gathered, precision=HIGH, preferred_element_type=F32)
        group = lane_ids((32, 128)) // 32
        own = jnp.zeros((32, 128), F32)
        for a in range(4):
            own = own + jnp.where(group == a, picked[32 * a:32 * a + 32], 0.0)
        own = own + pltpu.roll(own, 32, 1)
        own = own + pltpu.roll(own, 64, 1)
        group = lane_ids((8, 128)) // 32
        ordered = jnp.zeros((8, 128), F32)
        for q in range(4):
            ordered = ordered + jnp.where(group == q, own[8 * q:8 * q + 8], 0.0)
        for c in range(4):
            acc = inv[128 * c:128 * c + 128, 0:128] * ordered[0:1]
            for i in range(1, 8):
                acc = acc + inv[128 * c:128 * c + 128, 128 * i:128 * i + 128] * ordered[i:i + 1]
            csend[n, c:c + 1] = row_sums(acc)[0:1]

    def prolong(n):
        slot = slot_ref[gx * ny + gy]
        row = cbuf[n, slot // 16, pl.ds((slot // 4) % 4, 1), :]
        row = jnp.where(lane // 32 == slot % 4, row, 0.0)
        row = row + pltpu.roll(row, 32, 1)
        row = row + pltpu.roll(row, 64, 1)
        row = row * live
        total = jnp.zeros((8, 16, 128), F32)
        for k in range(kmax):
            weight = jnp.broadcast_to(row[:, k:k + 1], (1, 128)).reshape(1, 1, 128)
            total = total + vec[k].astype(F32) * weight
        return total

    rho = [1.0 / SIGMA]
    for _ in range(2):
        rho.append(1.0 / (2.0 * SIGMA - rho[-1]))

    def smooth_update(n, update, rest):
        return rho[n] * rho[n - 1] * update + (2.0 * rho[n] / DELTA) * jac[...] * rest

    def scalar(row, i):
        return jnp.broadcast_to(row[:, i:i + 1], (1, 128)).reshape(1, 1, 128)

    loads[0].wait()
    loads[1].wait()
    stack[...] = jnp.zeros((128, 128), F32)
    project(0, right, [])
    loads[2].wait()
    loads[3].wait()
    fl = 1.0 - solid[...].astype(F32)
    fluid[...] = fl
    jac[...] = 1.0 / (fl * (6.0 + diag[...]) + 1.0 - fl)
    pad[...] = jnp.zeros(pad.shape, F32)

    pl.semaphore_wait(barrier, nx - 1 + ny - 1)
    z_start(0)

    def apply_preconditioner(n, res, h, between=None):
        update = jac[...] * res / THETA
        halo_start(h, update)
        if n == 0:
            block = gy // 2
            want = lax.broadcasted_iota(jnp.int32, (32, 128), 0)
            want = 32 * block + 4 * (want % 8) + want // 8
            for a in range(4):
                have = slots_ref[pl.ds(128 * a, 128)].reshape(1, 128)
                onehot[32 * a:32 * a + 32, :] = (want == have).astype(F32)
        rest = res - halo_finish(h, update)
        smooth = update
        update = smooth_update(1, update, rest)
        smooth = smooth + update
        halo_start(h + 1, update)
        wait_bytes(zbuf.at[n], z_recv_sem.at[n])
        compact(n)
        p_start(n)
        rest = rest - halo_finish(h + 1, update)
        smooth = smooth + smooth_update(2, update, rest)
        if n == 0:
            loads[4].wait()
        wait_bytes(pbuf.at[n], p_recv_sem.at[n])
        coarse(n)
        c_start(n)
        sums = jnp.sum(pbuf[n, 4], axis=0, keepdims=True)
        wait_bytes(cbuf.at[n], c_recv_sem.at[n])
        return smooth + prolong(n), sums

    r0 = right[...]
    z0, _ = apply_preconditioner(0, r0, 0)
    sol_ref[...] = z0
    halo_start(2, z0)
    norm_part = fold(r0 * z0)
    q0 = halo_finish(2, z0)
    res_ref[...] = q0
    project(1, res_ref, [norm_part, fold(z0 * q0)])
    z_start(1)
    w0, sums = apply_preconditioner(1, q0, 3)
    norm0, curv0 = scalar(sums, kmax), scalar(sums, kmax + 1)
    step0 = norm0 / curv0
    z0, q0 = sol_ref[...], res_ref[...]
    z1 = z0 - step0 * w0
    r1 = right[...] - step0 * q0
    right[...] = r1
    halo_start(5, z1)
    parts[0] = fold(r1 * z1)
    parts[1] = fold(z1 * q0)
    t1 = halo_finish(5, z1)
    parts[2] = fold(z1 * t1)

    stack[0:8, :] = jnp.sum(parts[0:8], axis=1)
    fsend[...] = row_sums(stack[...])[0:1]
    for step in range(1, nx):
        remote(fsend, fzbuf.at[gx], f_send_sem.at[0], f_recv_sem.at[0], along_x(step)).start()
    pltpu.make_async_copy(fsend, fzbuf.at[gx], f_recv_sem.at[0]).start()
    wait_bytes(fzbuf, f_recv_sem.at[0])
    fpsend[...] = jnp.sum(fzbuf[...], axis=0)
    for step in range(1, ny):
        remote(fpsend, fpbuf.at[gy], f_send_sem.at[1], f_recv_sem.at[1], along_y(step)).start()
    pltpu.make_async_copy(fpsend, fpbuf.at[gy], f_recv_sem.at[1]).start()
    wait_bytes(fpbuf, f_recv_sem.at[1])
    last = jnp.sum(fpbuf[...], axis=0)
    norm1, cross, inner = scalar(last, 0), scalar(last, 1), scalar(last, 2)
    beta = norm1 / norm0
    step1 = norm1 / (inner + 2.0 * beta * cross + beta * beta * curv0)
    sol_ref[...] = (step0 + step1 * beta) * z0 + step1 * z1
    res_ref[...] = right[...] - step1 * (t1 + beta * q0)

    for n in range(2):
        wait_bytes(zbuf.at[n, pl.ds(0, nx - 1)], z_send_sem.at[n])
        wait_bytes(pbuf.at[n, :, pl.ds(0, ny - 1)], p_send_sem.at[n])
        wait_bytes(cbuf.at[n, pl.ds(0, ny - 1)], c_send_sem.at[n])
    for n in range(6):
        for copy in halo_copies(n):
            copy.wait_send()
    wait_bytes(fzbuf.at[pl.ds(0, nx - 1)], f_send_sem.at[0])
    wait_bytes(fpbuf.at[pl.ds(0, ny - 1)], f_send_sem.at[1])


def solution(mesh):
    nx, ny = mesh.shape["gx"], mesh.shape["gy"]

    def on_device(right_side, diagonal, solid_mask, vectors, counts, slots, inverse):
        cells = right_side.shape
        kmax = vectors.shape[0]
        hbm = pl.BlockSpec(memory_space=pl.ANY)
        smem = pl.BlockSpec(memory_space=pltpu.SMEM)
        vmem = pl.BlockSpec(memory_space=pltpu.VMEM)
        dma = pltpu.SemaphoreType.DMA
        out = jax.ShapeDtypeStruct(cells, F32)
        return pl.pallas_call(
            functools.partial(kernel, nx, ny, kmax),
            out_shape=(out, out),
            in_specs=[hbm, hbm, hbm, hbm, smem, smem, vmem, hbm],
            out_specs=(vmem, vmem),
            scratch_shapes=[
                pltpu.VMEM(cells, F32), pltpu.VMEM(cells, F32), pltpu.VMEM(cells, jnp.int32),
                pltpu.VMEM(vectors.shape, vectors.dtype), pltpu.VMEM(inverse.shape, F32),
                pltpu.VMEM(cells, F32), pltpu.VMEM(cells, F32), pltpu.VMEM((10, 32, 128), F32),
                pltpu.VMEM((kmax + 8, 8, 128), F32), pltpu.VMEM((128, 128), F32), pltpu.VMEM((128, 128), F32),
                pltpu.VMEM((2, 1, 128), F32), pltpu.VMEM((2, nx, 1, 128), F32),
                pltpu.VMEM((2, 5, 1, 128), F32), pltpu.VMEM((2, 5, ny, 128), F32),
                pltpu.VMEM((2, 4, 128), F32), pltpu.VMEM((2, ny, 4, 128), F32),
                pltpu.VMEM((6, 2, 16, 128), F32), pltpu.VMEM((6, 2, 16, 128), F32),
                pltpu.VMEM((6, 2, 8, 128), F32), pltpu.VMEM((6, 2, 8, 128), F32),
                pltpu.VMEM((1, 128), F32), pltpu.VMEM((nx, 1, 128), F32),
                pltpu.VMEM((1, 128), F32), pltpu.VMEM((ny, 1, 128), F32),
                dma((5,)), dma((2,)), dma((2,)), dma((2,)), dma((2,)), dma((2,)), dma((2,)),
                dma((6, 4)), dma((6, 4)), dma((2,)), dma((2,)),
            ],
            compiler_params=pltpu.CompilerParams(
                collective_id=0, has_side_effects=True, vmem_limit_bytes=32 * 1024 * 1024
            ),
            cost_estimate=pl.CostEstimate(flops=10_000_000, bytes_accessed=4_000_000, transcendentals=0),
        )(right_side, diagonal, solid_mask, vectors, counts, slots, slots, inverse)

    in_specs = (
        P("gx", "gy", None),
        P("gx", "gy", None),
        P("gx", "gy", None),
        P(None, "gx", "gy", None),
        P("gx", "gy"),
        P(),
        P("gy", None),
    )
    out_specs = (P("gx", "gy", None), P("gx", "gy", None))
    return jax.shard_map(
        on_device, mesh=mesh, in_specs=in_specs, out_specs=out_specs, check_vma=False
    )
```

```python
import functools

import jax
import jax.numpy as jnp
from jax import lax
from jax.experimental import pallas as pl
from jax.experimental.pallas import tpu as pltpu
from jax.sharding import PartitionSpec as P

CHEB_LO = 0.3
CHEB_HI = 2.0
THETA = (CHEB_HI + CHEB_LO) / 2.0
DELTA = (CHEB_HI - CHEB_LO) / 2.0
SIGMA = THETA / DELTA
HIGH = lax.Precision.HIGHEST
MESH = pl.DeviceIdType.MESH
F32 = jnp.float32


def lane_ids(shape):
    return lax.broadcasted_iota(jnp.int32, shape, len(shape) - 1)


def row_sums(rows):
    return lax.dot_general(
        jnp.ones((8, 128), F32), rows, (((1,), (1,)), ((), ())),
        precision=HIGH, preferred_element_type=F32,
    )


def kernel(
    nx, ny, kmax,
    right_hbm, diag_hbm, mask_hbm, vec_hbm, slots_hbm, inv_hbm,
    sol_ref, res_ref,
    right, diag, solid, vec, inv, fluid, jac, pad,
    parts, stack, onehot, slot_ref, slots_ref,
    zsend, zbuf, psend, pbuf, csend, cbuf,
    xsend, xbuf, ysend, ybuf,
    xface, xnear, yface, ynear, held,
    fsend, fzbuf, fpsend, fpbuf,
    load_sem, z_send_sem, z_recv_sem, p_send_sem, p_recv_sem, c_send_sem, c_recv_sem,
    h_send_sem, h_recv_sem, v_send_sem, v_recv_sem, f_send_sem, f_recv_sem,
):
    gx, gy = lax.axis_index("gx"), lax.axis_index("gy")

    def along_x(step):
        return {"gx": lax.rem(gx + step, nx)}

    def along_y(step):
        return {"gy": lax.rem(gy + step, ny)}

    barrier = pltpu.get_barrier_semaphore()
    for step in range(1, nx):
        pl.semaphore_signal(barrier, inc=1, device_id=along_x(step), device_id_type=MESH)
    for step in range(1, ny):
        pl.semaphore_signal(barrier, inc=1, device_id=along_y(step), device_id_type=MESH)

    loads = [
        pltpu.make_async_copy(src, dst, load_sem.at[i])
        for i, (src, dst) in enumerate(
            [(right_hbm, right), (vec_hbm, vec), (mask_hbm, solid), (diag_hbm, diag), (inv_hbm, inv),
             (slots_hbm, slot_ref), (slots_hbm, slots_ref)]
        )
    ]
    for load in loads:
        load.start()

    lane = lane_ids((1, 128))

    def remote(src, dst, send_sem, recv_sem, device):
        return pltpu.make_async_remote_copy(
            src_ref=src, dst_ref=dst, send_sem=send_sem, recv_sem=recv_sem,
            device_id=device, device_id_type=MESH,
        )

    def wait_bytes(ref, sem):
        pltpu.make_async_copy(ref, ref, sem).wait()

    def fold(cells):
        total = jnp.sum(cells, axis=0)
        return total[0:8] + total[8:16]

    def z_start(n):
        for step in range(1, nx):
            remote(zsend.at[n], zbuf.at[n, gx], z_send_sem.at[n], z_recv_sem.at[n], along_x(step)).start()
        pltpu.make_async_copy(zsend.at[n], zbuf.at[n, gx], z_recv_sem.at[n]).start()

    def p_start(n):
        for step in range(1, ny):
            remote(psend.at[n], pbuf.at[n, :, pl.ds(gy, 1)], p_send_sem.at[n], p_recv_sem.at[n], along_y(step)).start()
        pltpu.make_async_copy(psend.at[n], pbuf.at[n, :, pl.ds(gy, 1)], p_recv_sem.at[n]).start()

    def c_start(n):
        for step in range(1, ny):
            remote(csend.at[n], cbuf.at[n, gy], c_send_sem.at[n], c_recv_sem.at[n], along_y(step)).start()
        pltpu.make_async_copy(csend.at[n], cbuf.at[n, gy], c_recv_sem.at[n]).start()

    def halo_copies(n):
        return [
            remote(xsend.at[n, 0], xbuf.at[n, 1], h_send_sem.at[n, 0], h_recv_sem.at[n, 0], along_x(nx - 1)),
            remote(xsend.at[n, 1], xbuf.at[n, 0], h_send_sem.at[n, 1], h_recv_sem.at[n, 1], along_x(1)),
            remote(ysend.at[n, 0], ybuf.at[n, 1], h_send_sem.at[n, 2], h_recv_sem.at[n, 2], along_y(ny - 1)),
            remote(ysend.at[n, 1], ybuf.at[n, 0], h_send_sem.at[n, 3], h_recv_sem.at[n, 3], along_y(1)),
        ]

    def face_copies():
        return [
            remote(xface.at[0], xnear.at[1], v_send_sem.at[0], v_recv_sem.at[0], along_x(nx - 1)),
            remote(xface.at[1], xnear.at[0], v_send_sem.at[1], v_recv_sem.at[1], along_x(1)),
            remote(yface.at[0], ynear.at[1], v_send_sem.at[2], v_recv_sem.at[2], along_y(ny - 1)),
            remote(yface.at[1], ynear.at[0], v_send_sem.at[3], v_recv_sem.at[3], along_y(1)),
        ]

    def halo_start(n, field):
        masked = fluid[...] * field
        xsend[n, 0] = masked[0]
        xsend[n, 1] = masked[7]
        ysend[n, 0] = masked[:, 0, :]
        ysend[n, 1] = masked[:, 15, :]
        for copy in halo_copies(n):
            copy.start()

    def halo_finish(n):
        for copy in halo_copies(n):
            copy.wait_recv()
        return [xbuf[n, 0], xbuf[n, 1], ybuf[n, 0], ybuf[n, 1]]

    keep = [gx > 0, gx < nx - 1, gy > 0, gy < ny - 1]
    scale = [jnp.where(k, jnp.float32(1.0), jnp.float32(0.0)) for k in keep]

    def operate(field, halo):
        fl = fluid[...]
        masked = fl * field
        pad[1:9, 8:24, :] = masked
        pad[0, 8:24, :] = halo[0] * scale[0]
        pad[9, 8:24, :] = halo[1] * scale[1]
        pad[1:9, 7:8, :] = (halo[2] * scale[2]).reshape(8, 1, 128)
        pad[1:9, 24:25, :] = (halo[3] * scale[3]).reshape(8, 1, 128)
        beside = pad[2:10, 8:24, :] + pad[0:8, 8:24, :]
        beside = beside + pad[1:9, 9:25, :] + pad[1:9, 7:23, :]
        lanes = lane_ids((8, 16, 128))
        beside = beside + jnp.where(lanes == 127, 0.0, pltpu.roll(masked, 127, 2))
        beside = beside + jnp.where(lanes == 0, 0.0, pltpu.roll(masked, 1, 2))
        return fl * ((6.0 + diag[...]) * field - beside) + (1.0 - fl) * field

    def project(n, cells_ref, extras):
        def group(g, carry):
            cells = cells_ref[...]
            for j in range(4):
                k = g * 4 + j
                parts[k] = fold(vec[k].astype(F32) * cells)
            return carry

        lax.fori_loop(0, kmax // 4, group, 0)
        for i in range(8):
            parts[kmax + i] = extras[i] if i < len(extras) else jnp.zeros((8, 128), F32)
        stack[0:kmax + 8, :] = jnp.sum(parts[...], axis=1)
        zsend[n] = row_sums(stack[...])[0:1] * live

    def compact(n):
        rows = zbuf[n].reshape(nx, 128)
        low = jnp.where(lane_ids((nx, 128)) < kmax, rows, 0.0)
        packed = low[0:4]
        for a in range(1, 4):
            packed = packed + pltpu.roll(low[4 * a:4 * a + 4], 32 * a, 1)
        psend[n, 0:4] = packed.reshape(4, 1, 128)
        psend[n, 4] = jnp.sum(rows, axis=0, keepdims=True)

    def coarse(n):
        gathered = pbuf[n, 0:4].reshape(4 * ny, 128)
        picked = jnp.dot(onehot[...], gathered, precision=HIGH, preferred_element_type=F32)
        group = lane_ids((32, 128)) // 32
        own = jnp.zeros((32, 128), F32)
        for a in range(4):
            own = own + jnp.where(group == a, picked[32 * a:32 * a + 32], 0.0)
        own = own + pltpu.roll(own, 32, 1)
        own = own + pltpu.roll(own, 64, 1)
        group = lane_ids((8, 128)) // 32
        ordered = jnp.zeros((8, 128), F32)
        for q in range(4):
            ordered = ordered + jnp.where(group == q, own[8 * q:8 * q + 8], 0.0)
        for c in range(4):
            acc = inv[128 * c:128 * c + 128, 0:128] * ordered[0:1]
            for i in range(1, 8):
                acc = acc + inv[128 * c:128 * c + 128, 128 * i:128 * i + 128] * ordered[i:i + 1]
            csend[n, c:c + 1] = row_sums(acc)[0:1]

    def coefficients(n, sub_x, sub_y):
        slot = slot_ref[sub_x * ny + sub_y]
        row = cbuf[n, slot // 16, pl.ds((slot // 4) % 4, 1), :]
        row = jnp.where(lane // 32 == slot % 4, row, 0.0)
        row = row + pltpu.roll(row, 32, 1)
        return row + pltpu.roll(row, 64, 1)

    def prolong(n):
        own = coefficients(n, gx, gy) * live
        near = [
            coefficients(n, lax.rem(gx + nx - 1, nx), gy), coefficients(n, lax.rem(gx + 1, nx), gy),
            coefficients(n, gx, lax.rem(gy + ny - 1, ny)), coefficients(n, gx, lax.rem(gy + 1, ny)),
        ]
        total = jnp.zeros((8, 16, 128), F32)
        halo = [jnp.zeros((16, 128), F32), jnp.zeros((16, 128), F32), jnp.zeros((8, 128), F32), jnp.zeros((8, 128), F32)]
        for k in range(kmax):
            total = total + vec[k].astype(F32) * scalar(own, k).reshape(1, 1, 128)
        for k in range(kmax):
            for i in range(2):
                halo[i] = halo[i] + xnear[i, k] * scalar(near[i], k)
                halo[2 + i] = halo[2 + i] + ynear[i, k] * scalar(near[2 + i], k)
        return total, halo

    rho = [1.0 / SIGMA]
    for _ in range(2):
        rho.append(1.0 / (2.0 * SIGMA - rho[-1]))

    def smooth_update(n, update, rest):
        return rho[n] * rho[n - 1] * update + (2.0 * rho[n] / DELTA) * jac[...] * rest

    def scalar(row, i):
        return jnp.broadcast_to(row[:, i:i + 1], (1, 128))

    for i in (5, 6, 0, 1):
        loads[i].wait()
    live = ((lane < slot_ref[nx * ny]) | (lane >= kmax)).astype(F32)
    stack[...] = jnp.zeros((128, 128), F32)
    project(0, right, [])
    loads[2].wait()
    loads[3].wait()
    fl = 1.0 - solid[...].astype(F32)
    fluid[...] = fl
    jac[...] = 1.0 / (fl * (6.0 + diag[...]) + 1.0 - fl)
    pad[...] = jnp.zeros(pad.shape, F32)

    def faces(k, carry):
        alive = jnp.where(k < slot_ref[nx * ny], jnp.float32(1.0), jnp.float32(0.0))
        values = vec[k].astype(F32) * (fluid[...] * alive)
        xface[0, k] = values[0]
        xface[1, k] = values[7]
        yface[0, k] = values[:, 0, :]
        yface[1, k] = values[:, 15, :]
        return carry

    lax.fori_loop(0, kmax, faces, 0)

    pl.semaphore_wait(barrier, nx - 1 + ny - 1)
    z_start(0)

    def apply_preconditioner(n, res, h):
        update = jac[...] * res / THETA
        halo_start(h, update)
        if n == 0:
            for copy in face_copies()[2:]:
                copy.start()
            block = gy // 2
            want = lax.broadcasted_iota(jnp.int32, (32, 128), 0)
            want = 32 * block + 4 * (want % 8) + want // 8
            for a in range(4):
                have = slots_ref[pl.ds(128 * a, 128)].reshape(1, 128)
                onehot[32 * a:32 * a + 32, :] = (want == have).astype(F32)
        rest = res - operate(update, halo_finish(h))
        smooth = update
        update = smooth_update(1, update, rest)
        smooth = smooth + update
        halo_start(h + 1, update)
        wait_bytes(zbuf.at[n], z_recv_sem.at[n])
        compact(n)
        p_start(n)
        if n == 0:
            for copy in face_copies()[:2]:
                copy.start()
        rest = rest - operate(update, halo_finish(h + 1))
        smooth = smooth + smooth_update(2, update, rest)
        halo_start(h + 2, smooth)
        if n == 0:
            loads[4].wait()
        wait_bytes(pbuf.at[n], p_recv_sem.at[n])
        coarse(n)
        c_start(n)
        sums = jnp.sum(pbuf[n, 4], axis=0, keepdims=True)
        near = halo_finish(h + 2)
        if n == 0:
            for copy in face_copies():
                copy.wait_recv()
        wait_bytes(cbuf.at[n], c_recv_sem.at[n])
        fine, halo = prolong(n)
        return smooth + fine, [a + b for a, b in zip(near, halo)], sums

    r0 = right[...]
    z0, near, _ = apply_preconditioner(0, r0, 0)
    sol_ref[...] = z0
    held[0:16, :] = near[0]
    held[16:32, :] = near[1]
    held[32:40, :] = near[2]
    held[40:48, :] = near[3]
    q0 = operate(z0, near)
    res_ref[...] = q0
    project(1, res_ref, [fold(right[...] * z0), fold(z0 * q0)])
    z_start(1)
    w0, near, sums = apply_preconditioner(1, q0, 3)
    norm0, curv0 = scalar(sums, kmax), scalar(sums, kmax + 1)
    step0 = norm0 / curv0
    before = [held[0:16, :], held[16:32, :], held[32:40, :], held[40:48, :]]
    near = [a - step0 * b for a, b in zip(before, near)]
    norm0, curv0, step0 = (v.reshape(1, 1, 128) for v in (norm0, curv0, step0))
    z0, q0 = sol_ref[...], res_ref[...]
    z1 = z0 - step0 * w0
    r1 = right[...] - step0 * q0
    right[...] = r1
    parts[0] = fold(r1 * z1)
    parts[1] = fold(z1 * q0)
    t1 = operate(z1, near)
    parts[2] = fold(z1 * t1)

    stack[0:8, :] = jnp.sum(parts[0:8], axis=1)
    fsend[...] = row_sums(stack[...])[0:1]
    for step in range(1, nx):
        remote(fsend, fzbuf.at[gx], f_send_sem.at[0], f_recv_sem.at[0], along_x(step)).start()
    pltpu.make_async_copy(fsend, fzbuf.at[gx], f_recv_sem.at[0]).start()
    wait_bytes(fzbuf, f_recv_sem.at[0])
    fpsend[...] = jnp.sum(fzbuf[...], axis=0)
    for step in range(1, ny):
        remote(fpsend, fpbuf.at[gy], f_send_sem.at[1], f_recv_sem.at[1], along_y(step)).start()
    pltpu.make_async_copy(fpsend, fpbuf.at[gy], f_recv_sem.at[1]).start()
    wait_bytes(fpbuf, f_recv_sem.at[1])
    last = jnp.sum(fpbuf[...], axis=0)
    norm1, cross, inner = (scalar(last, i).reshape(1, 1, 128) for i in range(3))
    beta = norm1 / norm0
    step1 = norm1 / (inner + 2.0 * beta * cross + beta * beta * curv0)
    sol_ref[...] = (step0 + step1 * beta) * z0 + step1 * z1
    res_ref[...] = right[...] - step1 * (t1 + beta * q0)

    for n in range(2):
        wait_bytes(zbuf.at[n, pl.ds(0, nx - 1)], z_send_sem.at[n])
        wait_bytes(pbuf.at[n, :, pl.ds(0, ny - 1)], p_send_sem.at[n])
        wait_bytes(cbuf.at[n, pl.ds(0, ny - 1)], c_send_sem.at[n])
    for n in range(6):
        for copy in halo_copies(n):
            copy.wait_send()
    for copy in face_copies():
        copy.wait_send()
    wait_bytes(fzbuf.at[pl.ds(0, nx - 1)], f_send_sem.at[0])
    wait_bytes(fpbuf.at[pl.ds(0, ny - 1)], f_send_sem.at[1])


def solution(mesh):
    nx, ny = mesh.shape["gx"], mesh.shape["gy"]

    def on_device(right_side, diagonal, solid_mask, vectors, counts, slots, inverse):
        cells = right_side.shape
        kmax = vectors.shape[0]
        hbm = pl.BlockSpec(memory_space=pl.ANY)
        vmem = pl.BlockSpec(memory_space=pltpu.VMEM)
        dma = pltpu.SemaphoreType.DMA
        out = jax.ShapeDtypeStruct(cells, F32)
        slots = jnp.concatenate([slots, jnp.broadcast_to(counts.reshape(1), (128,))])
        return pl.pallas_call(
            functools.partial(kernel, nx, ny, kmax),
            out_shape=(out, out),
            in_specs=[hbm] * 6,
            out_specs=(vmem, vmem),
            scratch_shapes=[
                pltpu.VMEM(cells, F32), pltpu.VMEM(cells, F32), pltpu.VMEM(cells, jnp.int32),
                pltpu.VMEM(vectors.shape, vectors.dtype), pltpu.VMEM(inverse.shape, F32),
                pltpu.VMEM(cells, F32), pltpu.VMEM(cells, F32), pltpu.VMEM((10, 32, 128), F32),
                pltpu.VMEM((kmax + 8, 8, 128), F32), pltpu.VMEM((128, 128), F32), pltpu.VMEM((128, 128), F32),
                pltpu.SMEM(slots.shape, jnp.int32), pltpu.VMEM(slots.shape, jnp.int32),
                pltpu.VMEM((2, 1, 128), F32), pltpu.VMEM((2, nx, 1, 128), F32),
                pltpu.VMEM((2, 5, 1, 128), F32), pltpu.VMEM((2, 5, ny, 128), F32),
                pltpu.VMEM((2, 4, 128), F32), pltpu.VMEM((2, ny, 4, 128), F32),
                pltpu.VMEM((6, 2, 16, 128), F32), pltpu.VMEM((6, 2, 16, 128), F32),
                pltpu.VMEM((6, 2, 8, 128), F32), pltpu.VMEM((6, 2, 8, 128), F32),
                pltpu.VMEM((2, kmax, 16, 128), F32), pltpu.VMEM((2, kmax, 16, 128), F32),
                pltpu.VMEM((2, kmax, 8, 128), F32), pltpu.VMEM((2, kmax, 8, 128), F32), pltpu.VMEM((48, 128), F32),
                pltpu.VMEM((1, 128), F32), pltpu.VMEM((nx, 1, 128), F32),
                pltpu.VMEM((1, 128), F32), pltpu.VMEM((ny, 1, 128), F32),
                dma((7,)), dma((2,)), dma((2,)), dma((2,)), dma((2,)), dma((2,)), dma((2,)),
                dma((6, 4)), dma((6, 4)), dma((4,)), dma((4,)), dma((2,)), dma((2,)),
            ],
            compiler_params=pltpu.CompilerParams(
                collective_id=0, has_side_effects=True, vmem_limit_bytes=5375 * 1024 * 1024 // 100
            ),
            cost_estimate=pl.CostEstimate(flops=10_000_000, bytes_accessed=4_000_000, transcendentals=0),
        )(right_side, diagonal, solid_mask, vectors, slots, inverse)

    in_specs = (
        P("gx", "gy", None),
        P("gx", "gy", None),
        P("gx", "gy", None),
        P(None, "gx", "gy", None),
        P("gx", "gy"),
        P(),
        P("gy", None),
    )
    out_specs = (P("gx", "gy", None), P("gx", "gy", None))
    return jax.shard_map(
        on_device, mesh=mesh, in_specs=in_specs, out_specs=out_specs, check_vma=False
    )
```

```python
import functools

import jax
import jax.numpy as jnp
from jax import lax
from jax.experimental import pallas as pl
from jax.experimental.pallas import tpu as pltpu
from jax.sharding import PartitionSpec as P

CHEB_LO = 0.3
CHEB_HI = 2.0
THETA = (CHEB_HI + CHEB_LO) / 2.0
DELTA = (CHEB_HI - CHEB_LO) / 2.0
SIGMA = THETA / DELTA
MESH = pl.DeviceIdType.MESH
F32 = jnp.float32
BF16 = jnp.bfloat16


def lane_ids(shape):
    return lax.broadcasted_iota(jnp.int32, shape, len(shape) - 1)


def pieces(values):
    high = values.astype(BF16)
    rest = values - high.astype(F32)
    middle = rest.astype(BF16)
    return high, middle, (rest - middle.astype(F32)).astype(BF16)


def row_sums(rows):
    ones = jnp.ones((16, 128), BF16)
    return sum(
        lax.dot_general(ones, piece, (((1,), (1,)), ((), ())), preferred_element_type=F32)
        for piece in pieces(rows)
    )


def spread_sums(rows):
    ones = jnp.ones((128, 128), BF16)
    return sum(jnp.dot(piece, ones, preferred_element_type=F32) for piece in pieces(rows))


def kernel(
    nx, ny, kmax,
    right_hbm, diag_hbm, mask_hbm, vec_hbm, slots_hbm, inv_hbm,
    sol_ref, res_ref,
    right, diag, solid, vec, inv, fluid, jac, pad,
    parts, stack, onehot, coef, slot_ref, slots_ref,
    zsend, zbuf, psend, pbuf, csend, cbuf,
    xsend, xbuf, ysend, ybuf,
    xface, xnear, yface, ynear, held,
    fsend, fzbuf, fpsend, fpbuf,
    load_sem, z_send_sem, z_recv_sem, p_send_sem, p_recv_sem, c_send_sem, c_recv_sem,
    h_send_sem, h_recv_sem, v_send_sem, v_recv_sem, f_send_sem, f_recv_sem,
):
    gx, gy = lax.axis_index("gx"), lax.axis_index("gy")

    def along_x(step):
        return {"gx": lax.rem(gx + step, nx)}

    def along_y(step):
        return {"gy": lax.rem(gy + step, ny)}

    barrier = pltpu.get_barrier_semaphore()
    for step in range(1, nx):
        pl.semaphore_signal(barrier, inc=1, device_id=along_x(step), device_id_type=MESH)
    for step in range(1, ny):
        pl.semaphore_signal(barrier, inc=1, device_id=along_y(step), device_id_type=MESH)

    loads = [
        pltpu.make_async_copy(src, dst, load_sem.at[i])
        for i, (src, dst) in enumerate(
            [(right_hbm, right), (vec_hbm, vec), (mask_hbm, solid), (diag_hbm, diag), (inv_hbm, inv),
             (slots_hbm, slot_ref), (slots_hbm, slots_ref)]
        )
    ]
    for load in loads:
        load.start()

    lane = lane_ids((1, 128))

    def remote(src, dst, send_sem, recv_sem, device):
        return pltpu.make_async_remote_copy(
            src_ref=src, dst_ref=dst, send_sem=send_sem, recv_sem=recv_sem,
            device_id=device, device_id_type=MESH,
        )

    def wait_bytes(ref, sem):
        pltpu.make_async_copy(ref, ref, sem).wait()

    def fold(cells):
        total = jnp.sum(cells, axis=0)
        return total[0:8] + total[8:16]

    def z_start(n):
        for step in range(1, nx):
            remote(zsend.at[n], zbuf.at[n, gx], z_send_sem.at[n], z_recv_sem.at[n], along_x(step)).start()
        pltpu.make_async_copy(zsend.at[n], zbuf.at[n, gx], z_recv_sem.at[n]).start()

    def p_start(n):
        for step in range(1, ny):
            remote(psend.at[n], pbuf.at[n, :, pl.ds(gy, 1)], p_send_sem.at[n], p_recv_sem.at[n], along_y(step)).start()
        pltpu.make_async_copy(psend.at[n], pbuf.at[n, :, pl.ds(gy, 1)], p_recv_sem.at[n]).start()

    def c_start(n):
        for step in range(1, ny):
            remote(csend.at[n], cbuf.at[n, gy], c_send_sem.at[n], c_recv_sem.at[n], along_y(step)).start()
        pltpu.make_async_copy(csend.at[n], cbuf.at[n, gy], c_recv_sem.at[n]).start()

    def halo_copies(n):
        return [
            remote(xsend.at[n, 0], xbuf.at[n, 1], h_send_sem.at[n, 0], h_recv_sem.at[n, 0], along_x(nx - 1)),
            remote(xsend.at[n, 1], xbuf.at[n, 0], h_send_sem.at[n, 1], h_recv_sem.at[n, 1], along_x(1)),
            remote(ysend.at[n, 0], ybuf.at[n, 1], h_send_sem.at[n, 2], h_recv_sem.at[n, 2], along_y(ny - 1)),
            remote(ysend.at[n, 1], ybuf.at[n, 0], h_send_sem.at[n, 3], h_recv_sem.at[n, 3], along_y(1)),
        ]

    def face_copies():
        return [
            remote(xface.at[0], xnear.at[1], v_send_sem.at[0], v_recv_sem.at[0], along_x(nx - 1)),
            remote(xface.at[1], xnear.at[0], v_send_sem.at[1], v_recv_sem.at[1], along_x(1)),
            remote(yface.at[0], ynear.at[1], v_send_sem.at[2], v_recv_sem.at[2], along_y(ny - 1)),
            remote(yface.at[1], ynear.at[0], v_send_sem.at[3], v_recv_sem.at[3], along_y(1)),
        ]

    def halo_start(n, field):
        masked = fluid[...] * field
        xsend[n, 0] = masked[0]
        xsend[n, 1] = masked[7]
        ysend[n, 0] = masked[:, 0, :]
        ysend[n, 1] = masked[:, 15, :]
        for copy in halo_copies(n):
            copy.start()

    def halo_finish(n):
        for copy in halo_copies(n):
            copy.wait_recv()
        return [xbuf[n, 0], xbuf[n, 1], ybuf[n, 0], ybuf[n, 1]]

    keep = [gx > 0, gx < nx - 1, gy > 0, gy < ny - 1]
    scale = [jnp.where(k, jnp.float32(1.0), jnp.float32(0.0)) for k in keep]

    def operate(field, halo):
        fl = fluid[...]
        masked = fl * field
        pad[1:9, 8:24, :] = masked
        pad[0, 8:24, :] = halo[0] * scale[0]
        pad[9, 8:24, :] = halo[1] * scale[1]
        pad[1:9, 7:8, :] = (halo[2] * scale[2]).reshape(8, 1, 128)
        pad[1:9, 24:25, :] = (halo[3] * scale[3]).reshape(8, 1, 128)
        beside = pad[2:10, 8:24, :] + pad[0:8, 8:24, :]
        beside = beside + pad[1:9, 9:25, :] + pad[1:9, 7:23, :]
        lanes = lane_ids((8, 16, 128))
        beside = beside + jnp.where(lanes == 127, 0.0, pltpu.roll(masked, 127, 2))
        beside = beside + jnp.where(lanes == 0, 0.0, pltpu.roll(masked, 1, 2))
        return fl * ((6.0 + diag[...]) * field - beside) + (1.0 - fl) * field

    def project(n, cells_ref, extras):
        def group(g, carry):
            cells = cells_ref[...]
            for j in range(4):
                k = g * 4 + j
                parts[k] = fold(vec[k].astype(F32) * cells)
            return carry

        lax.fori_loop(0, kmax // 4, group, 0)
        for i in range(8):
            parts[kmax + i] = extras[i] if i < len(extras) else jnp.zeros((8, 128), F32)
        stack[0:kmax + 8, :] = jnp.sum(parts[...], axis=1)
        zsend[n] = row_sums(stack[...])[0:1] * live

    def compact(n):
        rows = zbuf[n].reshape(nx, 128)
        low = jnp.where(lane_ids((nx, 128)) < kmax, rows, 0.0)
        packed = low[0:4]
        for a in range(1, 4):
            packed = packed + pltpu.roll(low[4 * a:4 * a + 4], 32 * a, 1)
        psend[n, 0:4] = packed.reshape(4, 1, 128)
        psend[n, 4] = jnp.sum(rows, axis=0, keepdims=True)

    def coarse(n):
        gathered = pbuf[n, 0:4].reshape(4 * ny, 128)
        picked = sum(jnp.dot(onehot[...], piece, preferred_element_type=F32) for piece in pieces(gathered))
        group = lane_ids((32, 128)) // 32
        own = jnp.zeros((32, 128), F32)
        for a in range(4):
            own = own + jnp.where(group == a, picked[32 * a:32 * a + 32], 0.0)
        own = own + pltpu.roll(own, 32, 1)
        own = own + pltpu.roll(own, 64, 1)
        group = lane_ids((8, 128)) // 32
        ordered = jnp.zeros((8, 128), F32)
        for q in range(4):
            ordered = ordered + jnp.where(group == q, own[8 * q:8 * q + 8], 0.0)
        for c in range(4):
            acc = inv[128 * c:128 * c + 128, 0:128] * ordered[0:1]
            for i in range(1, 8):
                acc = acc + inv[128 * c:128 * c + 128, 128 * i:128 * i + 128] * ordered[i:i + 1]
            csend[n, c:c + 1] = row_sums(acc)[0:1]

    def coefficients(n, sub_x, sub_y, limit):
        slot = slot_ref[sub_x * ny + sub_y]
        row = cbuf[n, slot // 16, pl.ds((slot // 4) % 4, 1), :]
        k = lax.broadcasted_iota(jnp.int32, (kmax, 128), 0)
        mine = (lane_ids((kmax, 128)) == kmax * (slot % 4) + k) & (k < limit)
        return jnp.where(mine, row, 0.0)

    def prolong(n):
        subs = [
            (gx, gy, slot_ref[nx * ny]),
            (lax.rem(gx + nx - 1, nx), gy, kmax), (lax.rem(gx + 1, nx), gy, kmax),
            (gx, lax.rem(gy + ny - 1, ny), kmax), (gx, lax.rem(gy + 1, ny), kmax),
        ]
        coef[...] = spread_sums(jnp.concatenate([coefficients(n, *sub) for sub in subs], axis=0))

        def weight(i, k):
            return coef[i * kmax + k:i * kmax + k + 1, :]

        total = jnp.zeros((8, 16, 128), F32)
        halo = [jnp.zeros((16, 128), F32), jnp.zeros((16, 128), F32), jnp.zeros((8, 128), F32), jnp.zeros((8, 128), F32)]
        for k in range(kmax):
            total = total + vec[k].astype(F32) * weight(0, k).reshape(1, 1, 128)
        for k in range(kmax):
            for i in range(2):
                halo[i] = halo[i] + xnear[i, k] * weight(1 + i, k)
                halo[2 + i] = halo[2 + i] + ynear[i, k] * weight(3 + i, k)
        return total, halo

    rho = [1.0 / SIGMA]
    for _ in range(2):
        rho.append(1.0 / (2.0 * SIGMA - rho[-1]))

    def smooth_update(n, update, rest):
        return rho[n] * rho[n - 1] * update + (2.0 * rho[n] / DELTA) * jac[...] * rest

    def scalar(row, i):
        return jnp.broadcast_to(row[:, i:i + 1], (1, 128))

    for i in (5, 6, 0, 1):
        loads[i].wait()
    live = ((lane < slot_ref[nx * ny]) | (lane >= kmax)).astype(F32)
    stack[...] = jnp.zeros((128, 128), F32)
    project(0, right, [])
    loads[2].wait()
    loads[3].wait()
    fl = 1.0 - solid[...].astype(F32)
    fluid[...] = fl
    jac[...] = 1.0 / (fl * (6.0 + diag[...]) + 1.0 - fl)
    pad[...] = jnp.zeros(pad.shape, F32)

    def faces(k, carry):
        alive = jnp.where(k < slot_ref[nx * ny], jnp.float32(1.0), jnp.float32(0.0))
        values = vec[k].astype(F32) * (fluid[...] * alive)
        xface[0, k] = values[0]
        xface[1, k] = values[7]
        yface[0, k] = values[:, 0, :]
        yface[1, k] = values[:, 15, :]
        return carry

    lax.fori_loop(0, kmax, faces, 0)

    pl.semaphore_wait(barrier, nx - 1 + ny - 1)
    z_start(0)

    def apply_preconditioner(n, res, h):
        update = jac[...] * res / THETA
        halo_start(h, update)
        if n == 0:
            for copy in face_copies()[2:]:
                copy.start()
            block = gy // 2
            want = lax.broadcasted_iota(jnp.int32, (32, 128), 0)
            want = 32 * block + 4 * (want % 8) + want // 8
            for a in range(4):
                have = slots_ref[pl.ds(128 * a, 128)].reshape(1, 128)
                onehot[32 * a:32 * a + 32, :] = (want == have).astype(F32).astype(BF16)
        rest = res - operate(update, halo_finish(h))
        smooth = update
        update = smooth_update(1, update, rest)
        smooth = smooth + update
        halo_start(h + 1, update)
        wait_bytes(zbuf.at[n], z_recv_sem.at[n])
        compact(n)
        p_start(n)
        if n == 0:
            for copy in face_copies()[:2]:
                copy.start()
        rest = rest - operate(update, halo_finish(h + 1))
        smooth = smooth + smooth_update(2, update, rest)
        halo_start(h + 2, smooth)
        if n == 0:
            loads[4].wait()
        wait_bytes(pbuf.at[n], p_recv_sem.at[n])
        coarse(n)
        c_start(n)
        sums = jnp.sum(pbuf[n, 4], axis=0, keepdims=True)
        near = halo_finish(h + 2)
        if n == 0:
            for copy in face_copies():
                copy.wait_recv()
        wait_bytes(cbuf.at[n], c_recv_sem.at[n])
        fine, halo = prolong(n)
        return smooth + fine, [a + b for a, b in zip(near, halo)], sums

    r0 = right[...]
    z0, near, _ = apply_preconditioner(0, r0, 0)
    sol_ref[...] = z0
    held[0:16, :] = near[0]
    held[16:32, :] = near[1]
    held[32:40, :] = near[2]
    held[40:48, :] = near[3]
    q0 = operate(z0, near)
    res_ref[...] = q0
    project(1, res_ref, [fold(right[...] * z0), fold(z0 * q0)])
    z_start(1)
    w0, near, sums = apply_preconditioner(1, q0, 3)
    norm0, curv0 = scalar(sums, kmax), scalar(sums, kmax + 1)
    step0 = norm0 / curv0
    before = [held[0:16, :], held[16:32, :], held[32:40, :], held[40:48, :]]
    near = [a - step0 * b for a, b in zip(before, near)]
    norm0, curv0, step0 = (v.reshape(1, 1, 128) for v in (norm0, curv0, step0))
    z0, q0 = sol_ref[...], res_ref[...]
    z1 = z0 - step0 * w0
    r1 = right[...] - step0 * q0
    right[...] = r1
    parts[0] = fold(r1 * z1)
    parts[1] = fold(z1 * q0)
    t1 = operate(z1, near)
    parts[2] = fold(z1 * t1)

    stack[0:8, :] = jnp.sum(parts[0:8], axis=1)
    fsend[...] = row_sums(stack[...])[0:1]
    for step in range(1, nx):
        remote(fsend, fzbuf.at[gx], f_send_sem.at[0], f_recv_sem.at[0], along_x(step)).start()
    pltpu.make_async_copy(fsend, fzbuf.at[gx], f_recv_sem.at[0]).start()
    wait_bytes(fzbuf, f_recv_sem.at[0])
    fpsend[...] = jnp.sum(fzbuf[...], axis=0)
    for step in range(1, ny):
        remote(fpsend, fpbuf.at[gy], f_send_sem.at[1], f_recv_sem.at[1], along_y(step)).start()
    pltpu.make_async_copy(fpsend, fpbuf.at[gy], f_recv_sem.at[1]).start()
    wait_bytes(fpbuf, f_recv_sem.at[1])
    last = jnp.sum(fpbuf[...], axis=0)
    norm1, cross, inner = (scalar(last, i).reshape(1, 1, 128) for i in range(3))
    beta = norm1 / norm0
    step1 = norm1 / (inner + 2.0 * beta * cross + beta * beta * curv0)
    sol_ref[...] = (step0 + step1 * beta) * z0 + step1 * z1
    res_ref[...] = right[...] - step1 * (t1 + beta * q0)

    for n in range(2):
        wait_bytes(zbuf.at[n, pl.ds(0, nx - 1)], z_send_sem.at[n])
        wait_bytes(pbuf.at[n, :, pl.ds(0, ny - 1)], p_send_sem.at[n])
        wait_bytes(cbuf.at[n, pl.ds(0, ny - 1)], c_send_sem.at[n])
    for n in range(6):
        for copy in halo_copies(n):
            copy.wait_send()
    for copy in face_copies():
        copy.wait_send()
    wait_bytes(fzbuf.at[pl.ds(0, nx - 1)], f_send_sem.at[0])
    wait_bytes(fpbuf.at[pl.ds(0, ny - 1)], f_send_sem.at[1])


def solution(mesh):
    nx, ny = mesh.shape["gx"], mesh.shape["gy"]

    def on_device(right_side, diagonal, solid_mask, vectors, counts, slots, inverse):
        cells = right_side.shape
        kmax = vectors.shape[0]
        hbm = pl.BlockSpec(memory_space=pl.ANY)
        vmem = pl.BlockSpec(memory_space=pltpu.VMEM)
        dma = pltpu.SemaphoreType.DMA
        out = jax.ShapeDtypeStruct(cells, F32)
        slots = jnp.concatenate([slots, jnp.broadcast_to(counts.reshape(1), (128,))])
        return pl.pallas_call(
            functools.partial(kernel, nx, ny, kmax),
            out_shape=(out, out),
            in_specs=[hbm] * 6,
            out_specs=(vmem, vmem),
            scratch_shapes=[
                pltpu.VMEM(cells, F32), pltpu.VMEM(cells, F32), pltpu.VMEM(cells, jnp.int32),
                pltpu.VMEM(vectors.shape, vectors.dtype), pltpu.VMEM(inverse.shape, F32),
                pltpu.VMEM(cells, F32), pltpu.VMEM(cells, F32), pltpu.VMEM((10, 32, 128), F32),
                pltpu.VMEM((kmax + 8, 8, 128), F32), pltpu.VMEM((128, 128), F32), pltpu.VMEM((128, 128), BF16), pltpu.VMEM((5 * kmax, 128), F32),
                pltpu.SMEM(slots.shape, jnp.int32), pltpu.VMEM(slots.shape, jnp.int32),
                pltpu.VMEM((2, 1, 128), F32), pltpu.VMEM((2, nx, 1, 128), F32),
                pltpu.VMEM((2, 5, 1, 128), F32), pltpu.VMEM((2, 5, ny, 128), F32),
                pltpu.VMEM((2, 4, 128), F32), pltpu.VMEM((2, ny, 4, 128), F32),
                pltpu.VMEM((6, 2, 16, 128), F32), pltpu.VMEM((6, 2, 16, 128), F32),
                pltpu.VMEM((6, 2, 8, 128), F32), pltpu.VMEM((6, 2, 8, 128), F32),
                pltpu.VMEM((2, kmax, 16, 128), F32), pltpu.VMEM((2, kmax, 16, 128), F32),
                pltpu.VMEM((2, kmax, 8, 128), F32), pltpu.VMEM((2, kmax, 8, 128), F32), pltpu.VMEM((48, 128), F32),
                pltpu.VMEM((1, 128), F32), pltpu.VMEM((nx, 1, 128), F32),
                pltpu.VMEM((1, 128), F32), pltpu.VMEM((ny, 1, 128), F32),
                dma((7,)), dma((2,)), dma((2,)), dma((2,)), dma((2,)), dma((2,)), dma((2,)),
                dma((6, 4)), dma((6, 4)), dma((4,)), dma((4,)), dma((2,)), dma((2,)),
            ],
            compiler_params=pltpu.CompilerParams(
                collective_id=0, has_side_effects=True, vmem_limit_bytes=5375 * 1024 * 1024 // 100
            ),
            cost_estimate=pl.CostEstimate(flops=10_000_000, bytes_accessed=4_000_000, transcendentals=0),
        )(right_side, diagonal, solid_mask, vectors, slots, inverse)

    in_specs = (
        P("gx", "gy", None),
        P("gx", "gy", None),
        P("gx", "gy", None),
        P(None, "gx", "gy", None),
        P("gx", "gy"),
        P(),
        P("gy", None),
    )
    out_specs = (P("gx", "gy", None), P("gx", "gy", None))
    return jax.shard_map(
        on_device, mesh=mesh, in_specs=in_specs, out_specs=out_specs, check_vma=False
    )
```

```python
import functools

import jax
import jax.numpy as jnp
from jax import lax
from jax.experimental import pallas as pl
from jax.experimental.pallas import tpu as pltpu
from jax.sharding import PartitionSpec as P

CHEB_LO = 0.3
CHEB_HI = 2.0
THETA = (CHEB_HI + CHEB_LO) / 2.0
DELTA = (CHEB_HI - CHEB_LO) / 2.0
SIGMA = THETA / DELTA
MESH = pl.DeviceIdType.MESH
F32 = jnp.float32
BF16 = jnp.bfloat16


def lane_ids(shape):
    return lax.broadcasted_iota(jnp.int32, shape, len(shape) - 1)


def pieces(values):
    high = values.astype(BF16)
    rest = values - high.astype(F32)
    middle = rest.astype(BF16)
    return high, middle, (rest - middle.astype(F32)).astype(BF16)


def row_sums(rows):
    ones = jnp.ones((16, 128), BF16)
    return sum(
        lax.dot_general(ones, piece, (((1,), (1,)), ((), ())), preferred_element_type=F32)
        for piece in pieces(rows)
    )


def spread_sums(rows):
    ones = jnp.ones((128, 128), BF16)
    return sum(jnp.dot(piece, ones, preferred_element_type=F32) for piece in pieces(rows))


def kernel(
    nx, ny, kmax,
    right_hbm, diag_hbm, mask_hbm, vec_hbm, slots_hbm, inv_hbm,
    sol_ref, res_ref,
    right, diag, solid, vec, inv, fluid, jac, pad,
    parts, stack, onehot, coef, slot_ref, slots_ref,
    zsend, zbuf, psend, pbuf, csend, cbuf,
    xsend, xbuf, ysend, ybuf,
    xface, xnear, yface, ynear, held,
    fsend, fzbuf, fpsend, fpbuf,
    load_sem, z_send_sem, z_recv_sem, p_send_sem, p_recv_sem, c_send_sem, c_recv_sem,
    h_send_sem, h_recv_sem, v_send_sem, v_recv_sem, f_send_sem, f_recv_sem,
):
    gx, gy = lax.axis_index("gx"), lax.axis_index("gy")

    def along_x(step):
        return {"gx": lax.rem(gx + step, nx)}

    def along_y(step):
        return {"gy": lax.rem(gy + step, ny)}

    barrier = pltpu.get_barrier_semaphore()
    for step in range(1, nx):
        pl.semaphore_signal(barrier, inc=1, device_id=along_x(step), device_id_type=MESH)
    for step in range(1, ny):
        pl.semaphore_signal(barrier, inc=1, device_id=along_y(step), device_id_type=MESH)

    loads = [
        pltpu.make_async_copy(src, dst, load_sem.at[i])
        for i, (src, dst) in enumerate(
            [(right_hbm, right), (vec_hbm, vec), (mask_hbm, solid), (diag_hbm, diag), (inv_hbm, inv),
             (slots_hbm, slot_ref), (slots_hbm, slots_ref)]
        )
    ]
    for load in loads:
        load.start()

    lane = lane_ids((1, 128))

    def remote(src, dst, send_sem, recv_sem, device):
        return pltpu.make_async_remote_copy(
            src_ref=src, dst_ref=dst, send_sem=send_sem, recv_sem=recv_sem,
            device_id=device, device_id_type=MESH,
        )

    def wait_bytes(ref, sem):
        pltpu.make_async_copy(ref, ref, sem).wait()

    def fold(cells):
        total = jnp.sum(cells, axis=0)
        return total[0:8] + total[8:16]

    def z_start(n):
        for step in range(1, nx):
            remote(zsend.at[n], zbuf.at[n, gx], z_send_sem.at[n], z_recv_sem.at[n], along_x(step)).start()
        pltpu.make_async_copy(zsend.at[n], zbuf.at[n, gx], z_recv_sem.at[n]).start()

    def p_start(n):
        for step in range(1, ny):
            remote(psend.at[n], pbuf.at[n, :, pl.ds(gy, 1)], p_send_sem.at[n], p_recv_sem.at[n], along_y(step)).start()
        pltpu.make_async_copy(psend.at[n], pbuf.at[n, :, pl.ds(gy, 1)], p_recv_sem.at[n]).start()

    def c_start(n):
        for step in range(1, ny):
            remote(csend.at[n], cbuf.at[n, gy], c_send_sem.at[n], c_recv_sem.at[n], along_y(step)).start()
        pltpu.make_async_copy(csend.at[n], cbuf.at[n, gy], c_recv_sem.at[n]).start()

    def halo_copies(n):
        return [
            remote(xsend.at[n, 0], xbuf.at[n, 1], h_send_sem.at[n, 0], h_recv_sem.at[n, 0], along_x(nx - 1)),
            remote(xsend.at[n, 1], xbuf.at[n, 0], h_send_sem.at[n, 1], h_recv_sem.at[n, 1], along_x(1)),
            remote(ysend.at[n, 0], ybuf.at[n, 1], h_send_sem.at[n, 2], h_recv_sem.at[n, 2], along_y(ny - 1)),
            remote(ysend.at[n, 1], ybuf.at[n, 0], h_send_sem.at[n, 3], h_recv_sem.at[n, 3], along_y(1)),
        ]

    def face_copies():
        return [
            remote(xface.at[0], xnear.at[1], v_send_sem.at[0], v_recv_sem.at[0], along_x(nx - 1)),
            remote(xface.at[1], xnear.at[0], v_send_sem.at[1], v_recv_sem.at[1], along_x(1)),
            remote(yface.at[0], ynear.at[1], v_send_sem.at[2], v_recv_sem.at[2], along_y(ny - 1)),
            remote(yface.at[1], ynear.at[0], v_send_sem.at[3], v_recv_sem.at[3], along_y(1)),
        ]

    def halo_start(n, field):
        masked = fluid[...] * field
        xsend[n, 0] = masked[0]
        xsend[n, 1] = masked[7]
        ysend[n, 0] = masked[:, 0, :]
        ysend[n, 1] = masked[:, 15, :]
        for copy in halo_copies(n):
            copy.start()

    def halo_finish(n):
        for copy in halo_copies(n):
            copy.wait_recv()
        return [xbuf[n, 0], xbuf[n, 1], ybuf[n, 0], ybuf[n, 1]]

    keep = [gx > 0, gx < nx - 1, gy > 0, gy < ny - 1]
    scale = [jnp.where(k, jnp.float32(1.0), jnp.float32(0.0)) for k in keep]

    def operate(field, halo):
        fl = fluid[...]
        masked = fl * field
        pad[1:9, 8:24, :] = masked
        pad[0, 8:24, :] = halo[0] * scale[0]
        pad[9, 8:24, :] = halo[1] * scale[1]
        pad[1:9, 7:8, :] = (halo[2] * scale[2]).reshape(8, 1, 128)
        pad[1:9, 24:25, :] = (halo[3] * scale[3]).reshape(8, 1, 128)
        beside = pad[2:10, 8:24, :] + pad[0:8, 8:24, :]
        beside = beside + pad[1:9, 9:25, :] + pad[1:9, 7:23, :]
        lanes = lane_ids((8, 16, 128))
        beside = beside + jnp.where(lanes == 127, 0.0, pltpu.roll(masked, 127, 2))
        beside = beside + jnp.where(lanes == 0, 0.0, pltpu.roll(masked, 1, 2))
        return fl * ((6.0 + diag[...]) * field - beside) + (1.0 - fl) * field

    def project(n, cells_ref, extras):
        cells = cells_ref[...]
        for k in range(kmax):
            parts[k] = fold(vec[k].astype(F32) * cells)
        for i in range(8):
            parts[kmax + i] = extras[i] if i < len(extras) else jnp.zeros((8, 128), F32)
        stack[0:kmax + 8, :] = jnp.sum(parts[...], axis=1)
        zsend[n] = row_sums(stack[...])[0:1] * live

    def compact(n):
        rows = zbuf[n].reshape(nx, 128)
        low = jnp.where(lane_ids((nx, 128)) < kmax, rows, 0.0)
        packed = low[0:4]
        for a in range(1, 4):
            packed = packed + pltpu.roll(low[4 * a:4 * a + 4], 32 * a, 1)
        psend[n, 0:4] = packed.reshape(4, 1, 128)
        psend[n, 4] = jnp.sum(rows, axis=0, keepdims=True)

    def coarse(n):
        gathered = pbuf[n, 0:4].reshape(4 * ny, 128)
        picked = sum(jnp.dot(onehot[...], piece, preferred_element_type=F32) for piece in pieces(gathered))
        group = lane_ids((32, 128)) // 32
        own = jnp.zeros((32, 128), F32)
        for a in range(4):
            own = own + jnp.where(group == a, picked[32 * a:32 * a + 32], 0.0)
        own = own + pltpu.roll(own, 32, 1)
        own = own + pltpu.roll(own, 64, 1)
        group = lane_ids((8, 128)) // 32
        ordered = jnp.zeros((8, 128), F32)
        for q in range(4):
            ordered = ordered + jnp.where(group == q, own[8 * q:8 * q + 8], 0.0)
        for c in range(4):
            acc = inv[128 * c:128 * c + 128, 0:128] * ordered[0:1]
            for i in range(1, 8):
                acc = acc + inv[128 * c:128 * c + 128, 128 * i:128 * i + 128] * ordered[i:i + 1]
            csend[n, c:c + 1] = row_sums(acc)[0:1]

    def coefficients(n, sub_x, sub_y, limit):
        slot = slot_ref[sub_x * ny + sub_y]
        row = cbuf[n, slot // 16, pl.ds((slot // 4) % 4, 1), :]
        k = lax.broadcasted_iota(jnp.int32, (kmax, 128), 0)
        mine = (lane_ids((kmax, 128)) == kmax * (slot % 4) + k) & (k < limit)
        return jnp.where(mine, row, 0.0)

    def prolong(n):
        subs = [
            (gx, gy, slot_ref[nx * ny]),
            (lax.rem(gx + nx - 1, nx), gy, kmax), (lax.rem(gx + 1, nx), gy, kmax),
            (gx, lax.rem(gy + ny - 1, ny), kmax), (gx, lax.rem(gy + 1, ny), kmax),
        ]
        coef[...] = spread_sums(jnp.concatenate([coefficients(n, *sub) for sub in subs], axis=0))

        def weight(i, k):
            return coef[i * kmax + k:i * kmax + k + 1, :]

        total = jnp.zeros((8, 16, 128), F32)
        halo = [jnp.zeros((16, 128), F32), jnp.zeros((16, 128), F32), jnp.zeros((8, 128), F32), jnp.zeros((8, 128), F32)]
        for k in range(kmax):
            total = total + vec[k].astype(F32) * weight(0, k).reshape(1, 1, 128)
        for k in range(kmax):
            for i in range(2):
                halo[i] = halo[i] + xnear[i, k] * weight(1 + i, k)
                halo[2 + i] = halo[2 + i] + ynear[i, k] * weight(3 + i, k)
        return total, halo

    rho = [1.0 / SIGMA]
    for _ in range(2):
        rho.append(1.0 / (2.0 * SIGMA - rho[-1]))

    def smooth_update(n, update, rest):
        return rho[n] * rho[n - 1] * update + (2.0 * rho[n] / DELTA) * jac[...] * rest

    def scalar(row, i):
        return jnp.broadcast_to(row[:, i:i + 1], (1, 128))

    for i in (5, 6, 0, 1):
        loads[i].wait()
    live = ((lane < slot_ref[nx * ny]) | (lane >= kmax)).astype(F32)
    stack[...] = jnp.zeros((128, 128), F32)
    project(0, right, [])
    loads[2].wait()
    loads[3].wait()
    fl = 1.0 - solid[...].astype(F32)
    fluid[...] = fl
    jac[...] = 1.0 / (fl * (6.0 + diag[...]) + 1.0 - fl)
    pad[...] = jnp.zeros(pad.shape, F32)

    def faces(k, carry):
        alive = jnp.where(k < slot_ref[nx * ny], jnp.float32(1.0), jnp.float32(0.0))
        values = vec[k].astype(F32) * (fluid[...] * alive)
        xface[0, k] = values[0]
        xface[1, k] = values[7]
        yface[0, k] = values[:, 0, :]
        yface[1, k] = values[:, 15, :]
        return carry

    lax.fori_loop(0, kmax, faces, 0)

    pl.semaphore_wait(barrier, nx - 1 + ny - 1)
    z_start(0)

    def apply_preconditioner(n, res, h):
        update = jac[...] * res / THETA
        halo_start(h, update)
        if n == 0:
            for copy in face_copies()[2:]:
                copy.start()
            block = gy // 2
            want = lax.broadcasted_iota(jnp.int32, (32, 128), 0)
            want = 32 * block + 4 * (want % 8) + want // 8
            for a in range(4):
                have = slots_ref[pl.ds(128 * a, 128)].reshape(1, 128)
                onehot[32 * a:32 * a + 32, :] = (want == have).astype(F32).astype(BF16)
        rest = res - operate(update, halo_finish(h))
        smooth = update
        update = smooth_update(1, update, rest)
        smooth = smooth + update
        halo_start(h + 1, update)
        wait_bytes(zbuf.at[n], z_recv_sem.at[n])
        compact(n)
        p_start(n)
        if n == 0:
            for copy in face_copies()[:2]:
                copy.start()
        rest = rest - operate(update, halo_finish(h + 1))
        smooth = smooth + smooth_update(2, update, rest)
        halo_start(h + 2, smooth)
        if n == 0:
            loads[4].wait()
        wait_bytes(pbuf.at[n], p_recv_sem.at[n])
        coarse(n)
        c_start(n)
        sums = jnp.sum(pbuf[n, 4], axis=0, keepdims=True)
        near = halo_finish(h + 2)
        if n == 0:
            for copy in face_copies():
                copy.wait_recv()
        wait_bytes(cbuf.at[n], c_recv_sem.at[n])
        fine, halo = prolong(n)
        return smooth + fine, [a + b for a, b in zip(near, halo)], sums

    r0 = right[...]
    z0, near, _ = apply_preconditioner(0, r0, 0)
    sol_ref[...] = z0
    held[0:16, :] = near[0]
    held[16:32, :] = near[1]
    held[32:40, :] = near[2]
    held[40:48, :] = near[3]
    q0 = operate(z0, near)
    res_ref[...] = q0
    project(1, res_ref, [fold(right[...] * z0), fold(z0 * q0)])
    z_start(1)
    w0, near, sums = apply_preconditioner(1, q0, 3)
    norm0, curv0 = scalar(sums, kmax), scalar(sums, kmax + 1)
    step0 = norm0 / curv0
    before = [held[0:16, :], held[16:32, :], held[32:40, :], held[40:48, :]]
    near = [a - step0 * b for a, b in zip(before, near)]
    norm0, curv0, step0 = (v.reshape(1, 1, 128) for v in (norm0, curv0, step0))
    z0, q0 = sol_ref[...], res_ref[...]
    z1 = z0 - step0 * w0
    r1 = right[...] - step0 * q0
    right[...] = r1
    parts[0] = fold(r1 * z1)
    parts[1] = fold(z1 * q0)
    t1 = operate(z1, near)
    parts[2] = fold(z1 * t1)

    stack[0:8, :] = jnp.sum(parts[0:8], axis=1)
    fsend[...] = row_sums(stack[...])[0:1]
    for step in range(1, nx):
        remote(fsend, fzbuf.at[gx], f_send_sem.at[0], f_recv_sem.at[0], along_x(step)).start()
    pltpu.make_async_copy(fsend, fzbuf.at[gx], f_recv_sem.at[0]).start()
    wait_bytes(fzbuf, f_recv_sem.at[0])
    fpsend[...] = jnp.sum(fzbuf[...], axis=0)
    for step in range(1, ny):
        remote(fpsend, fpbuf.at[gy], f_send_sem.at[1], f_recv_sem.at[1], along_y(step)).start()
    pltpu.make_async_copy(fpsend, fpbuf.at[gy], f_recv_sem.at[1]).start()
    wait_bytes(fpbuf, f_recv_sem.at[1])
    last = jnp.sum(fpbuf[...], axis=0)
    norm1, cross, inner = (scalar(last, i).reshape(1, 1, 128) for i in range(3))
    beta = norm1 / norm0
    step1 = norm1 / (inner + 2.0 * beta * cross + beta * beta * curv0)
    sol_ref[...] = (step0 + step1 * beta) * z0 + step1 * z1
    res_ref[...] = right[...] - step1 * (t1 + beta * q0)

    for n in range(2):
        wait_bytes(zbuf.at[n, pl.ds(0, nx - 1)], z_send_sem.at[n])
        wait_bytes(pbuf.at[n, :, pl.ds(0, ny - 1)], p_send_sem.at[n])
        wait_bytes(cbuf.at[n, pl.ds(0, ny - 1)], c_send_sem.at[n])
    for n in range(6):
        for copy in halo_copies(n):
            copy.wait_send()
    for copy in face_copies():
        copy.wait_send()
    wait_bytes(fzbuf.at[pl.ds(0, nx - 1)], f_send_sem.at[0])
    wait_bytes(fpbuf.at[pl.ds(0, ny - 1)], f_send_sem.at[1])


def solution(mesh):
    nx, ny = mesh.shape["gx"], mesh.shape["gy"]

    def on_device(right_side, diagonal, solid_mask, vectors, counts, slots, inverse):
        cells = right_side.shape
        kmax = vectors.shape[0]
        hbm = pl.BlockSpec(memory_space=pl.ANY)
        vmem = pl.BlockSpec(memory_space=pltpu.VMEM)
        dma = pltpu.SemaphoreType.DMA
        out = jax.ShapeDtypeStruct(cells, F32)
        slots = jnp.concatenate([slots, jnp.broadcast_to(counts.reshape(1), (128,))])
        return pl.pallas_call(
            functools.partial(kernel, nx, ny, kmax),
            out_shape=(out, out),
            in_specs=[hbm] * 6,
            out_specs=(vmem, vmem),
            scratch_shapes=[
                pltpu.VMEM(cells, F32), pltpu.VMEM(cells, F32), pltpu.VMEM(cells, jnp.int32),
                pltpu.VMEM(vectors.shape, vectors.dtype), pltpu.VMEM(inverse.shape, F32),
                pltpu.VMEM(cells, F32), pltpu.VMEM(cells, F32), pltpu.VMEM((10, 32, 128), F32),
                pltpu.VMEM((kmax + 8, 8, 128), F32), pltpu.VMEM((128, 128), F32), pltpu.VMEM((128, 128), BF16), pltpu.VMEM((5 * kmax, 128), F32),
                pltpu.SMEM(slots.shape, jnp.int32), pltpu.VMEM(slots.shape, jnp.int32),
                pltpu.VMEM((2, 1, 128), F32), pltpu.VMEM((2, nx, 1, 128), F32),
                pltpu.VMEM((2, 5, 1, 128), F32), pltpu.VMEM((2, 5, ny, 128), F32),
                pltpu.VMEM((2, 4, 128), F32), pltpu.VMEM((2, ny, 4, 128), F32),
                pltpu.VMEM((6, 2, 16, 128), F32), pltpu.VMEM((6, 2, 16, 128), F32),
                pltpu.VMEM((6, 2, 8, 128), F32), pltpu.VMEM((6, 2, 8, 128), F32),
                pltpu.VMEM((2, kmax, 16, 128), F32), pltpu.VMEM((2, kmax, 16, 128), F32),
                pltpu.VMEM((2, kmax, 8, 128), F32), pltpu.VMEM((2, kmax, 8, 128), F32), pltpu.VMEM((48, 128), F32),
                pltpu.VMEM((1, 128), F32), pltpu.VMEM((nx, 1, 128), F32),
                pltpu.VMEM((1, 128), F32), pltpu.VMEM((ny, 1, 128), F32),
                dma((7,)), dma((2,)), dma((2,)), dma((2,)), dma((2,)), dma((2,)), dma((2,)),
                dma((6, 4)), dma((6, 4)), dma((4,)), dma((4,)), dma((2,)), dma((2,)),
            ],
            compiler_params=pltpu.CompilerParams(
                collective_id=0, has_side_effects=True, vmem_limit_bytes=5375 * 1024 * 1024 // 100
            ),
            cost_estimate=pl.CostEstimate(flops=10_000_000, bytes_accessed=4_000_000, transcendentals=0),
        )(right_side, diagonal, solid_mask, vectors, slots, inverse)

    in_specs = (
        P("gx", "gy", None),
        P("gx", "gy", None),
        P("gx", "gy", None),
        P(None, "gx", "gy", None),
        P("gx", "gy"),
        P(),
        P("gy", None),
    )
    out_specs = (P("gx", "gy", None), P("gx", "gy", None))
    return jax.shard_map(
        on_device, mesh=mesh, in_specs=in_specs, out_specs=out_specs, check_vma=False
    )
```

```python
import functools

import jax
import jax.numpy as jnp
from jax import lax
from jax.experimental import pallas as pl
from jax.experimental.pallas import tpu as pltpu
from jax.sharding import PartitionSpec as P

CHEB_LO = 0.3
CHEB_HI = 2.0
THETA = (CHEB_HI + CHEB_LO) / 2.0
DELTA = (CHEB_HI - CHEB_LO) / 2.0
SIGMA = THETA / DELTA
MESH = pl.DeviceIdType.MESH
F32 = jnp.float32
BF16 = jnp.bfloat16


def lane_ids(shape):
    return lax.broadcasted_iota(jnp.int32, shape, len(shape) - 1)


def pieces(values):
    high = values.astype(BF16)
    rest = values - high.astype(F32)
    middle = rest.astype(BF16)
    return high, middle, (rest - middle.astype(F32)).astype(BF16)


def spread_sums(rows):
    ones = jnp.ones((128, 128), BF16)
    return sum(jnp.dot(piece, ones, preferred_element_type=F32) for piece in pieces(rows))


def row_sums(rows):
    diagonal = lane_ids((128, 128)) == lax.broadcasted_iota(jnp.int32, (128, 128), 0)
    return jnp.sum(jnp.where(diagonal, spread_sums(rows), 0.0), axis=0, keepdims=True)


def kernel(
    nx, ny, kmax,
    right_hbm, diag_hbm, mask_hbm, vec_hbm, slots_hbm, inv_hbm,
    sol_ref, res_ref,
    right, diag, solid, vec, inv, fluid, jac, pad,
    parts, stack, onehot, coef, slot_ref, slots_ref,
    zsend, zbuf, psend, pbuf, csend, cbuf,
    xsend, xbuf, ysend, ybuf,
    xface, xnear, yface, ynear, held,
    fsend, fzbuf, fpsend, fpbuf,
    load_sem, z_send_sem, z_recv_sem, p_send_sem, p_recv_sem, c_send_sem, c_recv_sem,
    h_send_sem, h_recv_sem, v_send_sem, v_recv_sem, f_send_sem, f_recv_sem,
):
    gx, gy = lax.axis_index("gx"), lax.axis_index("gy")

    def along_x(step):
        return {"gx": lax.rem(gx + step, nx)}

    def along_y(step):
        return {"gy": lax.rem(gy + step, ny)}

    barrier = pltpu.get_barrier_semaphore()
    for step in range(1, nx):
        pl.semaphore_signal(barrier, inc=1, device_id=along_x(step), device_id_type=MESH)
    for step in range(1, ny):
        pl.semaphore_signal(barrier, inc=1, device_id=along_y(step), device_id_type=MESH)

    loads = [
        pltpu.make_async_copy(src, dst, load_sem.at[i])
        for i, (src, dst) in enumerate(
            [(right_hbm, right), (vec_hbm, vec), (mask_hbm, solid), (diag_hbm, diag), (inv_hbm, inv),
             (slots_hbm, slot_ref), (slots_hbm, slots_ref)]
        )
    ]
    for load in loads:
        load.start()

    lane = lane_ids((1, 128))

    def remote(src, dst, send_sem, recv_sem, device):
        return pltpu.make_async_remote_copy(
            src_ref=src, dst_ref=dst, send_sem=send_sem, recv_sem=recv_sem,
            device_id=device, device_id_type=MESH,
        )

    def wait_bytes(ref, sem):
        pltpu.make_async_copy(ref, ref, sem).wait()

    def fold(cells):
        total = jnp.sum(cells, axis=0)
        return total[0:8] + total[8:16]

    def z_start(n):
        for step in range(1, nx):
            remote(zsend.at[n], zbuf.at[n, gx], z_send_sem.at[n], z_recv_sem.at[n], along_x(step)).start()
        pltpu.make_async_copy(zsend.at[n], zbuf.at[n, gx], z_recv_sem.at[n]).start()

    def p_start(n):
        for step in range(1, ny):
            remote(psend.at[n], pbuf.at[n, :, pl.ds(gy, 1)], p_send_sem.at[n], p_recv_sem.at[n], along_y(step)).start()
        pltpu.make_async_copy(psend.at[n], pbuf.at[n, :, pl.ds(gy, 1)], p_recv_sem.at[n]).start()

    def c_start(n):
        for step in range(1, ny):
            remote(csend.at[n], cbuf.at[n, gy], c_send_sem.at[n], c_recv_sem.at[n], along_y(step)).start()
        pltpu.make_async_copy(csend.at[n], cbuf.at[n, gy], c_recv_sem.at[n]).start()

    def halo_copies(n):
        return [
            remote(xsend.at[n, 0], xbuf.at[n, 1], h_send_sem.at[n, 0], h_recv_sem.at[n, 0], along_x(nx - 1)),
            remote(xsend.at[n, 1], xbuf.at[n, 0], h_send_sem.at[n, 1], h_recv_sem.at[n, 1], along_x(1)),
            remote(ysend.at[n, 0], ybuf.at[n, 1], h_send_sem.at[n, 2], h_recv_sem.at[n, 2], along_y(ny - 1)),
            remote(ysend.at[n, 1], ybuf.at[n, 0], h_send_sem.at[n, 3], h_recv_sem.at[n, 3], along_y(1)),
        ]

    def face_copies():
        return [
            remote(xface.at[0], xnear.at[1], v_send_sem.at[0], v_recv_sem.at[0], along_x(nx - 1)),
            remote(xface.at[1], xnear.at[0], v_send_sem.at[1], v_recv_sem.at[1], along_x(1)),
            remote(yface.at[0], ynear.at[1], v_send_sem.at[2], v_recv_sem.at[2], along_y(ny - 1)),
            remote(yface.at[1], ynear.at[0], v_send_sem.at[3], v_recv_sem.at[3], along_y(1)),
        ]

    def halo_start(n, field):
        masked = fluid[...] * field
        xsend[n, 0] = masked[0]
        xsend[n, 1] = masked[7]
        ysend[n, 0] = masked[:, 0, :]
        ysend[n, 1] = masked[:, 15, :]
        for copy in halo_copies(n):
            copy.start()

    def halo_finish(n):
        for copy in halo_copies(n):
            copy.wait_recv()
        return [xbuf[n, 0], xbuf[n, 1], ybuf[n, 0], ybuf[n, 1]]

    keep = [gx > 0, gx < nx - 1, gy > 0, gy < ny - 1]
    scale = [jnp.where(k, jnp.float32(1.0), jnp.float32(0.0)) for k in keep]

    def operate(field, halo):
        fl = fluid[...]
        masked = fl * field
        pad[1:9, 8:24, :] = masked
        pad[0, 8:24, :] = halo[0] * scale[0]
        pad[9, 8:24, :] = halo[1] * scale[1]
        pad[1:9, 7:8, :] = (halo[2] * scale[2]).reshape(8, 1, 128)
        pad[1:9, 24:25, :] = (halo[3] * scale[3]).reshape(8, 1, 128)
        beside = pad[2:10, 8:24, :] + pad[0:8, 8:24, :]
        beside = beside + pad[1:9, 9:25, :] + pad[1:9, 7:23, :]
        lanes = lane_ids((8, 16, 128))
        beside = beside + jnp.where(lanes == 127, 0.0, pltpu.roll(masked, 127, 2))
        beside = beside + jnp.where(lanes == 0, 0.0, pltpu.roll(masked, 1, 2))
        return fl * ((6.0 + diag[...]) * field - beside) + (1.0 - fl) * field

    def project(n, cells_ref, extras):
        cells = cells_ref[...]
        for k in range(kmax):
            parts[k] = fold(vec[k].astype(F32) * cells)
        for i in range(8):
            parts[kmax + i] = extras[i] if i < len(extras) else jnp.zeros((8, 128), F32)
        stack[0:kmax + 8, :] = jnp.sum(parts[...], axis=1)
        zsend[n] = row_sums(stack[...]) * live

    def compact(n):
        rows = zbuf[n].reshape(nx, 128)
        low = jnp.where(lane_ids((nx, 128)) < kmax, rows, 0.0)
        packed = low[0:4]
        for a in range(1, 4):
            packed = packed + pltpu.roll(low[4 * a:4 * a + 4], 32 * a, 1)
        psend[n, 0:4] = packed.reshape(4, 1, 128)
        psend[n, 4] = jnp.sum(rows, axis=0, keepdims=True)

    def coarse(n):
        gathered = pbuf[n, 0:4].reshape(4 * ny, 128)
        picked = sum(jnp.dot(onehot[...], piece, preferred_element_type=F32) for piece in pieces(gathered))
        group = lane_ids((32, 128)) // 32
        own = jnp.zeros((32, 128), F32)
        for a in range(4):
            own = own + jnp.where(group == a, picked[32 * a:32 * a + 32], 0.0)
        own = own + pltpu.roll(own, 32, 1)
        own = own + pltpu.roll(own, 64, 1)
        group = lane_ids((8, 128)) // 32
        ordered = jnp.zeros((8, 128), F32)
        for q in range(4):
            ordered = ordered + jnp.where(group == q, own[8 * q:8 * q + 8], 0.0)
        for c in range(4):
            acc = inv[128 * c:128 * c + 128, 0:128] * ordered[0:1]
            for i in range(1, 8):
                acc = acc + inv[128 * c:128 * c + 128, 128 * i:128 * i + 128] * ordered[i:i + 1]
            csend[n, c:c + 1] = row_sums(acc)

    def coefficients(n, sub_x, sub_y, limit):
        slot = slot_ref[sub_x * ny + sub_y]
        row = cbuf[n, slot // 16, pl.ds((slot // 4) % 4, 1), :]
        k = lax.broadcasted_iota(jnp.int32, (kmax, 128), 0)
        mine = (lane_ids((kmax, 128)) == kmax * (slot % 4) + k) & (k < limit)
        return jnp.where(mine, row, 0.0)

    def prolong(n):
        subs = [
            (gx, gy, slot_ref[nx * ny]),
            (lax.rem(gx + nx - 1, nx), gy, kmax), (lax.rem(gx + 1, nx), gy, kmax),
            (gx, lax.rem(gy + ny - 1, ny), kmax), (gx, lax.rem(gy + 1, ny), kmax),
        ]
        coef[...] = spread_sums(jnp.concatenate([coefficients(n, *sub) for sub in subs], axis=0))

        def weight(i, k):
            return coef[i * kmax + k:i * kmax + k + 1, :]

        total = jnp.zeros((8, 16, 128), F32)
        halo = [jnp.zeros((16, 128), F32), jnp.zeros((16, 128), F32), jnp.zeros((8, 128), F32), jnp.zeros((8, 128), F32)]
        for k in range(kmax):
            total = total + vec[k].astype(F32) * weight(0, k).reshape(1, 1, 128)
        for k in range(kmax):
            for i in range(2):
                halo[i] = halo[i] + xnear[i, k] * weight(1 + i, k)
                halo[2 + i] = halo[2 + i] + ynear[i, k] * weight(3 + i, k)
        return total, halo

    rho = [1.0 / SIGMA]
    for _ in range(2):
        rho.append(1.0 / (2.0 * SIGMA - rho[-1]))

    def smooth_update(n, update, rest):
        return rho[n] * rho[n - 1] * update + (2.0 * rho[n] / DELTA) * jac[...] * rest

    def scalar(row, i):
        return jnp.broadcast_to(row[:, i:i + 1], (1, 128))

    for i in (5, 6, 0, 1):
        loads[i].wait()
    live = ((lane < slot_ref[nx * ny]) | (lane >= kmax)).astype(F32)
    stack[...] = jnp.zeros((128, 128), F32)
    project(0, right, [])
    loads[2].wait()
    loads[3].wait()
    fl = 1.0 - solid[...].astype(F32)
    fluid[...] = fl
    jac[...] = 1.0 / (fl * (6.0 + diag[...]) + 1.0 - fl)
    pad[...] = jnp.zeros(pad.shape, F32)

    def faces(k, carry):
        alive = jnp.where(k < slot_ref[nx * ny], jnp.float32(1.0), jnp.float32(0.0))
        values = vec[k].astype(F32) * (fluid[...] * alive)
        xface[0, k] = values[0]
        xface[1, k] = values[7]
        yface[0, k] = values[:, 0, :]
        yface[1, k] = values[:, 15, :]
        return carry

    lax.fori_loop(0, kmax, faces, 0)

    pl.semaphore_wait(barrier, nx - 1 + ny - 1)
    z_start(0)

    def apply_preconditioner(n, res, h):
        update = jac[...] * res / THETA
        halo_start(h, update)
        if n == 0:
            for copy in face_copies()[2:]:
                copy.start()
            block = gy // 2
            want = lax.broadcasted_iota(jnp.int32, (32, 128), 0)
            want = 32 * block + 4 * (want % 8) + want // 8
            for a in range(4):
                have = slots_ref[pl.ds(128 * a, 128)].reshape(1, 128)
                onehot[32 * a:32 * a + 32, :] = (want == have).astype(F32).astype(BF16)
        rest = res - operate(update, halo_finish(h))
        smooth = update
        update = smooth_update(1, update, rest)
        smooth = smooth + update
        halo_start(h + 1, update)
        wait_bytes(zbuf.at[n], z_recv_sem.at[n])
        compact(n)
        p_start(n)
        if n == 0:
            for copy in face_copies()[:2]:
                copy.start()
        rest = rest - operate(update, halo_finish(h + 1))
        smooth = smooth + smooth_update(2, update, rest)
        halo_start(h + 2, smooth)
        if n == 0:
            loads[4].wait()
        wait_bytes(pbuf.at[n], p_recv_sem.at[n])
        coarse(n)
        c_start(n)
        sums = jnp.sum(pbuf[n, 4], axis=0, keepdims=True)
        near = halo_finish(h + 2)
        if n == 0:
            for copy in face_copies():
                copy.wait_recv()
        wait_bytes(cbuf.at[n], c_recv_sem.at[n])
        fine, halo = prolong(n)
        return smooth + fine, [a + b for a, b in zip(near, halo)], sums

    r0 = right[...]
    z0, near, _ = apply_preconditioner(0, r0, 0)
    sol_ref[...] = z0
    held[0:16, :] = near[0]
    held[16:32, :] = near[1]
    held[32:40, :] = near[2]
    held[40:48, :] = near[3]
    q0 = operate(z0, near)
    res_ref[...] = q0
    project(1, res_ref, [fold(right[...] * z0), fold(z0 * q0)])
    z_start(1)
    w0, near, sums = apply_preconditioner(1, q0, 3)
    norm0, curv0 = scalar(sums, kmax), scalar(sums, kmax + 1)
    step0 = norm0 / curv0
    before = [held[0:16, :], held[16:32, :], held[32:40, :], held[40:48, :]]
    near = [a - step0 * b for a, b in zip(before, near)]
    norm0, curv0, step0 = (v.reshape(1, 1, 128) for v in (norm0, curv0, step0))
    z0, q0 = sol_ref[...], res_ref[...]
    z1 = z0 - step0 * w0
    r1 = right[...] - step0 * q0
    right[...] = r1
    parts[0] = fold(r1 * z1)
    parts[1] = fold(z1 * q0)
    t1 = operate(z1, near)
    parts[2] = fold(z1 * t1)

    stack[0:8, :] = jnp.sum(parts[0:8], axis=1)
    fsend[...] = row_sums(stack[...])
    for step in range(1, nx):
        remote(fsend, fzbuf.at[gx], f_send_sem.at[0], f_recv_sem.at[0], along_x(step)).start()
    pltpu.make_async_copy(fsend, fzbuf.at[gx], f_recv_sem.at[0]).start()
    wait_bytes(fzbuf, f_recv_sem.at[0])
    fpsend[...] = jnp.sum(fzbuf[...], axis=0)
    for step in range(1, ny):
        remote(fpsend, fpbuf.at[gy], f_send_sem.at[1], f_recv_sem.at[1], along_y(step)).start()
    pltpu.make_async_copy(fpsend, fpbuf.at[gy], f_recv_sem.at[1]).start()
    wait_bytes(fpbuf, f_recv_sem.at[1])
    last = jnp.sum(fpbuf[...], axis=0)
    norm1, cross, inner = (scalar(last, i).reshape(1, 1, 128) for i in range(3))
    beta = norm1 / norm0
    step1 = norm1 / (inner + 2.0 * beta * cross + beta * beta * curv0)
    sol_ref[...] = (step0 + step1 * beta) * z0 + step1 * z1
    res_ref[...] = right[...] - step1 * (t1 + beta * q0)

    for n in range(2):
        wait_bytes(zbuf.at[n, pl.ds(0, nx - 1)], z_send_sem.at[n])
        wait_bytes(pbuf.at[n, :, pl.ds(0, ny - 1)], p_send_sem.at[n])
        wait_bytes(cbuf.at[n, pl.ds(0, ny - 1)], c_send_sem.at[n])
    for n in range(6):
        for copy in halo_copies(n):
            copy.wait_send()
    for copy in face_copies():
        copy.wait_send()
    wait_bytes(fzbuf.at[pl.ds(0, nx - 1)], f_send_sem.at[0])
    wait_bytes(fpbuf.at[pl.ds(0, ny - 1)], f_send_sem.at[1])


def solution(mesh):
    nx, ny = mesh.shape["gx"], mesh.shape["gy"]

    def on_device(right_side, diagonal, solid_mask, vectors, counts, slots, inverse):
        cells = right_side.shape
        kmax = vectors.shape[0]
        hbm = pl.BlockSpec(memory_space=pl.ANY)
        vmem = pl.BlockSpec(memory_space=pltpu.VMEM)
        dma = pltpu.SemaphoreType.DMA
        out = jax.ShapeDtypeStruct(cells, F32)
        slots = jnp.concatenate([slots, jnp.broadcast_to(counts.reshape(1), (128,))])
        return pl.pallas_call(
            functools.partial(kernel, nx, ny, kmax),
            out_shape=(out, out),
            in_specs=[hbm] * 6,
            out_specs=(vmem, vmem),
            scratch_shapes=[
                pltpu.VMEM(cells, F32), pltpu.VMEM(cells, F32), pltpu.VMEM(cells, jnp.int32),
                pltpu.VMEM(vectors.shape, vectors.dtype), pltpu.VMEM(inverse.shape, F32),
                pltpu.VMEM(cells, F32), pltpu.VMEM(cells, F32), pltpu.VMEM((10, 32, 128), F32),
                pltpu.VMEM((kmax + 8, 8, 128), F32), pltpu.VMEM((128, 128), F32), pltpu.VMEM((128, 128), BF16), pltpu.VMEM((5 * kmax, 128), F32),
                pltpu.SMEM(slots.shape, jnp.int32), pltpu.VMEM(slots.shape, jnp.int32),
                pltpu.VMEM((2, 1, 128), F32), pltpu.VMEM((2, nx, 1, 128), F32),
                pltpu.VMEM((2, 5, 1, 128), F32), pltpu.VMEM((2, 5, ny, 128), F32),
                pltpu.VMEM((2, 4, 128), F32), pltpu.VMEM((2, ny, 4, 128), F32),
                pltpu.VMEM((6, 2, 16, 128), F32), pltpu.VMEM((6, 2, 16, 128), F32),
                pltpu.VMEM((6, 2, 8, 128), F32), pltpu.VMEM((6, 2, 8, 128), F32),
                pltpu.VMEM((2, kmax, 16, 128), F32), pltpu.VMEM((2, kmax, 16, 128), F32),
                pltpu.VMEM((2, kmax, 8, 128), F32), pltpu.VMEM((2, kmax, 8, 128), F32), pltpu.VMEM((48, 128), F32),
                pltpu.VMEM((1, 128), F32), pltpu.VMEM((nx, 1, 128), F32),
                pltpu.VMEM((1, 128), F32), pltpu.VMEM((ny, 1, 128), F32),
                dma((7,)), dma((2,)), dma((2,)), dma((2,)), dma((2,)), dma((2,)), dma((2,)),
                dma((6, 4)), dma((6, 4)), dma((4,)), dma((4,)), dma((2,)), dma((2,)),
            ],
            compiler_params=pltpu.CompilerParams(
                collective_id=0, has_side_effects=True, vmem_limit_bytes=5375 * 1024 * 1024 // 100
            ),
            cost_estimate=pl.CostEstimate(flops=10_000_000, bytes_accessed=4_000_000, transcendentals=0),
        )(right_side, diagonal, solid_mask, vectors, slots, inverse)

    in_specs = (
        P("gx", "gy", None),
        P("gx", "gy", None),
        P("gx", "gy", None),
        P(None, "gx", "gy", None),
        P("gx", "gy"),
        P(),
        P("gy", None),
    )
    out_specs = (P("gx", "gy", None), P("gx", "gy", None))
    return jax.shard_map(
        on_device, mesh=mesh, in_specs=in_specs, out_specs=out_specs, check_vma=False
    )
```
